32 devices in a mesh: seq: 8 (over z, y), mp: 4 (over x, core).
Axes of the slice: x: 2, y: 2, z: 4, core: 2. Of those that a mesh axis runs over, the one named last changes fastest.
Arguments:
- tokens: bfloat16 [3072, 4096], P('seq', 'mp'), may hold values from -6 to 6
- norm_gain: float32 [2, 4096], replicated, may hold values from 0.25 to 1.75
- in_weight: bfloat16 [2, 3, 4096, 4096], P(None, None, 'seq', 'mp'), may hold values from -0.09375 to 0.09375
- feat_filter: float32 [2, 3, 3, 4096], P(None, None, None, 'mp'), may hold values from -3 to 3
- short_filter: float32 [256, 7], P('mp'), may hold values from -3 to 3
- medium_filter: float32 [256, 128], P('mp'), may hold values from -0.4 to 0.4
- out_weight: bfloat16 [4096, 4096], P('seq', 'mp'), may hold values from -0.09375 to 0.09375
Outputs:
- stream: bfloat16 [3072, 4096], P('seq', 'mp')
- mixed: bfloat16 [3072, 4096], P('seq', 'mp')
The draws below stay inside these ranges and needn't reach their ends.
All inputs are finite; a program needn't handle non-finite values.
Results may differ from the reference program's by a relative error of at most 0.015.
Values may be sent and summed in bfloat16 or wider, within the bound.
No kernel may reach another device: no remote copies, remote signals or barrier semaphores. Data moves between devices by JAX's collectives and lax.ppermute only.
A program may use at most 128 MiB of HBM per device.

```python
import math
import jax
import jax.numpy as jnp
from jax import lax

D = 4096
GROUP = 16
FEAT_TAPS = 3
SHORT = 7
MEDIUM = 128
GROUPS = 256
TOKENS = 3072


def draw_medium_filter(key, part):
    key_rate, key_noise = jax.random.split(key, 2)
    rate = jnp.exp(jax.random.uniform(key_rate, (GROUPS, 1), jnp.float32, math.log(0.003), math.log(0.1)))
    steps = jnp.arange(MEDIUM, dtype=jnp.float32)[None, :]
    noise = jax.random.truncated_normal(key_noise, -4.0, 4.0, (GROUPS, MEDIUM), jnp.float32)
    return 0.1 * noise * jnp.exp(-rate * steps)


def steps_of(own_key, extent, pieces, smallest, top_value):
    factor_of = 1.0
    for dim, shards_of in pieces:
        heights = jax.random.uniform(jax.random.fold_in(jax.random.fold_in(own_key, 6), dim), (shards_of,), jnp.float32, smallest / len(pieces), top_value / len(pieces))
        factor_of = factor_of * jnp.repeat(jnp.exp(heights), extent[dim] // shards_of).reshape((-1,) + (1,) * (len(extent) - 1 - dim))
    return factor_of


def bell_draw(key, dims, scale, most, cuts=(), kind=jnp.bfloat16):
    array = scale * jax.random.normal(key, dims, jnp.float32)
    if cuts:
        array = array * steps_of(key, dims, cuts, -0.22, 0.18)
    return jnp.clip(array, -most, most).astype(kind)


def setup_inputs(seed: int = 0) -> dict:
    streams_of = jax.random.split(jax.random.key(seed), 8)
    return {
        "tokens": bell_draw(streams_of[0], (TOKENS, D), 1.0, 6.0, ((0, 8), (1, 4))),
        "norm_gain": jnp.clip(1.0 + 0.15 * jax.random.normal(streams_of[1], (2, D), jnp.float32), 0.25, 1.75),
        "in_weight": bell_draw(streams_of[2], (2, 3, D, D), D ** -0.5, 0.09375, ((2, 8), (3, 4))),
        "feat_filter": bell_draw(streams_of[3], (2, 3, FEAT_TAPS, D), 0.5, 3.0, ((3, 4),), jnp.float32),
        "short_filter": bell_draw(streams_of[4], (GROUPS, SHORT), 0.35, 3.0, ((0, 4),), jnp.float32),
        "medium_filter": draw_medium_filter(jax.random.fold_in(streams_of[7], 71), 0),
        "out_weight": bell_draw(streams_of[6], (D, D), D ** -0.5, 0.09375, ((0, 8), (1, 4))),
    }


def rms_norm(stream_in, gain):
    values = stream_in.astype(jnp.float32)
    mean_sq = lax.optimization_barrier(jnp.mean(values * values, axis=-1, keepdims=True))
    return (values * lax.rsqrt(mean_sq + 1e-06) * gain).astype(jnp.bfloat16)

def causal_conv(signal, taps):
    count = taps.shape[0]
    length = signal.shape[0]
    padded = jnp.pad(signal, ((count - 1, 0), (0, 0)))

    def step(index, acc):
        start = (count - 1 - index).astype(jnp.int32)
        return acc + taps[index] * lax.dynamic_slice_in_dim(padded, start, length, 0)
    return lax.fori_loop(0, count, step, jnp.zeros_like(signal))

def hyena_block(stream_in, gain, weights, feat_taps, inner_taps):
    normed = rms_norm(stream_in, gain)
    proj = [jnp.dot(normed, weights[c], preferred_element_type=jnp.float32).astype(jnp.bfloat16) for c in range(3)]
    feat = [causal_conv(proj[c].astype(jnp.float32), feat_taps[c]) for c in range(3)]
    kv_prod = (feat[1] * feat[2]).astype(jnp.bfloat16)
    inner = causal_conv(kv_prod.astype(jnp.float32), inner_taps)
    return (feat[0] * inner).astype(jnp.bfloat16)

def reference(tokens, norm_gain, in_weight, feat_filter, short_filter, medium_filter, out_weight):
    short_taps = jnp.repeat(short_filter.T, GROUP, axis=1)
    medium_taps = jnp.repeat(medium_filter.T, GROUP, axis=1)
    first = hyena_block(tokens, norm_gain[0], in_weight[0], feat_filter[0], short_taps)
    stream = (tokens.astype(jnp.float32) + jnp.dot(first, out_weight, preferred_element_type=jnp.float32)).astype(jnp.bfloat16)
    mixed = hyena_block(stream, norm_gain[1], in_weight[1], feat_filter[1], medium_taps)
    return (stream, mixed)
```

```python
import functools

import jax
import jax.numpy as jnp
from jax import lax
from jax.experimental import pallas as pl
from jax.experimental.pallas import tpu as pltpu
from jax.sharding import Mesh, PartitionSpec as P

AXES = ("z", "y", "x", "c")


def factors(mesh):
    seq, mp = mesh.shape["seq"], mesh.shape["mp"]
    along_y = 1
    while 2 * along_y * along_y < seq:
        along_y *= 2
    return seq // along_y, along_y, mp // 2, 2


def rotate(value, axis, by):
    size = lax.axis_size(axis)
    return lax.ppermute(value, axis, [(i, (i + by) % size) for i in range(size)])


def split_kernel(place, *refs):
    del place
    gain = refs[0][...]
    half = (len(refs) - 1) // 2
    for source, target in zip(refs[1 : 1 + half], refs[1 + half :]):
        target[...] = (source[0, 0].astype(jnp.float32) * gain).astype(jnp.bfloat16)


def split_weights(in_weight, block, gain, z_at):
    parts = lax.axis_size("z")
    rows, columns = in_weight.shape[2], in_weight.shape[3] // parts
    if columns % 128:
        pieces = []
        for k in range(parts):
            begin = lax.rem(z_at + k, parts) * columns
            piece = lax.dynamic_slice_in_dim(in_weight[block], begin, columns, 2)
            piece = (piece.astype(jnp.float32) * gain).astype(jnp.bfloat16)
            pieces.append(piece.transpose(1, 0, 2).reshape(rows, 3 * columns))
        return pieces

    def source(k):
        return pl.BlockSpec((1, 1, rows, columns), lambda c, at: (block, c, 0, lax.rem(at[0] + k, parts)))

    return pl.pallas_call(
        split_kernel,
        grid_spec=pltpu.PrefetchScalarGridSpec(
            num_scalar_prefetch=1,
            grid=(3,),
            in_specs=[pl.BlockSpec((rows, 1), lambda c, at: (0, 0))] + [source(k) for k in range(parts)],
            out_specs=[pl.BlockSpec((rows, columns), lambda c, at: (0, c)) for _ in range(parts)],
        ),
        out_shape=[jax.ShapeDtypeStruct((rows, 3 * columns), jnp.bfloat16)] * parts,
    )(z_at[None], gain, *[in_weight] * parts)


def slot_of(z_from, x_at, c_at):
    x_size, c_size = lax.axis_size("x"), lax.axis_size("c")
    x_from, c_from = z_from // c_size, z_from % c_size
    return ((x_at - x_from) % x_size) * c_size + (c_at - c_from) % c_size


def over_y(pieces, where):
    z_at, y_at, x_at, c_at = where
    parts, y_size = lax.axis_size("z"), lax.axis_size("y")
    rows, columns = pieces[0].shape
    whole = jnp.zeros((parts, y_size, rows, columns), pieces[0].dtype)
    for k, piece in enumerate(pieces):
        slot = slot_of((z_at - k) % parts, x_at, c_at)
        for j in range(y_size):
            moved = rotate(piece, "y", j) if j else piece
            whole = lax.dynamic_update_slice(whole, moved[None, None], (slot, (y_at - j) % y_size, 0, 0))
    return whole.reshape(parts * y_size * rows, columns)


def all_features(piece):
    found = [piece] + [rotate(piece, "x", d) for d in range(1, lax.axis_size("x"))]
    return [rotate(p, "c", d) if d else p for p in found for d in range(lax.axis_size("c"))]


def ring(value):
    out = [value]
    for _ in range(lax.axis_size("z") - 1):
        out.append(rotate(out[-1], "z", 1))
    return out


def project(pieces, weights):
    out = []
    for piece in pieces:
        full = jnp.concatenate(all_features(piece), axis=1)
        values = full.astype(jnp.float32)
        scale = lax.rsqrt(jnp.mean(values * values, axis=-1, keepdims=True) + 1e-06)
        out.append((jnp.dot(full, weights, preferred_element_type=jnp.float32) * scale).astype(jnp.bfloat16))
    return out


def earlier_rows(pieces, count, z_at, y_at):
    parts, y_size = len(pieces), lax.axis_size("y")
    tails = [rotate(p[p.shape[0] - count :], "y", 1) for p in pieces]
    out = []
    for k in range(parts):
        wrapped = jnp.where(z_at == k, jnp.zeros_like(tails[k]), tails[(k + 1) % parts])
        out.append(jnp.where(y_at == 0, wrapped, tails[k]))
    return out


def causal(extended, taps, count):
    reach = taps.shape[0] - 1
    offset = extended.shape[0] - count - reach
    total = 0.0
    for index in range(reach + 1):
        begin = offset + reach - index
        total = total + taps[index] * extended[begin : begin + count]
    return total


def toeplitz_kernel(row_ref, out_ref):
    width = out_ref.shape[1]
    rows = jnp.broadcast_to(row_ref[0], (width, 3 * width))
    turned = pltpu.roll(rows, 0, 1, stride=1, stride_axis=0)
    out_ref[0] = turned[:, : 2 * width].astype(out_ref.dtype)


def toeplitz(filt):
    groups, width = filt.shape
    row = jnp.zeros((groups, 1, 3 * width), jnp.float32).at[:, 0, 1 : width + 1].set(filt[:, ::-1])
    return pl.pallas_call(
        toeplitz_kernel,
        grid=(groups,),
        in_specs=[pl.BlockSpec((1, 1, 3 * width), lambda g: (g, 0, 0))],
        out_specs=pl.BlockSpec((1, width, 2 * width), lambda g: (g, 0, 0)),
        out_shape=jax.ShapeDtypeStruct((groups, width, 2 * width), jnp.bfloat16),
    )(row)


def medium(extended, matrix):
    groups, width = matrix.shape[0], matrix.shape[1]
    blocks = extended.reshape(extended.shape[0] // width, width, groups, -1)
    pairs = jnp.concatenate([blocks[:-1], blocks[1:]], axis=1)
    out = jnp.einsum("gik,bkgc->bigc", matrix, pairs, preferred_element_type=jnp.float32)
    return out.reshape(out.shape[0] * width, -1)


def channels_of(value, z_at, axis):
    size = value.shape[axis] // lax.axis_size("z")
    return lax.dynamic_slice_in_dim(value, z_at * size, size, axis)


def home(pieces, z_at):
    parts = len(pieces)
    back = jnp.stack([rotate(p, "z", -k) if k else p for k, p in enumerate(pieces)])
    ordered = [lax.dynamic_index_in_dim(back, (j - z_at) % parts, 0, keepdims=False) for j in range(parts)]
    return jnp.concatenate(ordered, axis=1)


def local(tokens, norm_gain, in_weight, feat_filter, short_filter, medium_filter, out_weight):
    where = tuple(lax.axis_index(a) for a in AXES)
    z_at, y_at, x_at, c_at = where
    parts = lax.axis_size("z")
    rows = in_weight.shape[2]
    count = tokens.shape[0]
    width = in_weight.shape[3] // parts
    begin = (z_at * lax.axis_size("y") + y_at) * rows
    gains = lax.dynamic_slice_in_dim(norm_gain, begin, rows, 1)[:, :, None]
    feat = channels_of(feat_filter, z_at, 3)
    short = channels_of(short_filter, z_at, 0)
    short_taps = jnp.repeat(short.T, width // short.shape[0], axis=1)
    matrix = toeplitz(channels_of(medium_filter, z_at, 0))
    span = medium_filter.shape[1]
    reach = feat.shape[2] - 1

    def weights_of(block):
        pieces = split_weights(in_weight, block, gains[block], z_at)
        return over_y([rotate(p, "z", k) if k else p for k, p in enumerate(pieces)], where)

    def third(value, c):
        return value[:, c * width : (c + 1) * width].astype(jnp.float32)

    weights = weights_of(0)
    out_rows = over_y(ring(out_weight), where)
    weights_next = weights_of(1)

    proj = project(ring(tokens), weights)
    gated = []
    for piece, before in zip(proj, earlier_rows(proj, 8, z_at, y_at)):
        extended = jnp.concatenate([before, piece], axis=0)
        more = count + short_taps.shape[0] - 1
        query = causal(third(extended, 0), feat[0, 0], count)
        kv = causal(third(extended, 1), feat[0, 1], more) * causal(third(extended, 2), feat[0, 2], more)
        kv = kv.astype(jnp.bfloat16).astype(jnp.float32)
        gated.append((query * causal(kv, short_taps, count)).astype(jnp.bfloat16))
    first = jnp.concatenate(all_features(home(gated, z_at)), axis=1)
    delta = jnp.dot(first, out_rows, preferred_element_type=jnp.float32)
    stream = (tokens.astype(jnp.float32) + delta).astype(jnp.bfloat16)

    proj = project(ring(stream), weights_next)
    queries, kvs = [], []
    for piece, before in zip(proj, earlier_rows(proj, 8, z_at, y_at)):
        extended = jnp.concatenate([before, piece], axis=0)
        queries.append(causal(third(extended, 0), feat[1, 0], count))
        kv = causal(third(extended, 1), feat[1, 1], count) * causal(third(extended, 2), feat[1, 2], count)
        kvs.append(kv.astype(jnp.bfloat16))
    gated = []
    for query, kv, before in zip(queries, kvs, earlier_rows(kvs, span, z_at, y_at)):
        inner = medium(jnp.concatenate([before, kv], axis=0), matrix)
        gated.append((query * inner).astype(jnp.bfloat16))
    return stream, home(gated, z_at)


def solution(mesh):
    wide = Mesh(mesh.devices.reshape(factors(mesh)), AXES)
    seq, mp = ("z", "y"), ("x", "c")
    placed = (
        P(seq, mp),
        P(),
        P(None, None, seq, mp),
        P(None, None, None, mp),
        P(mp, None),
        P(mp, None),
        P(seq, mp),
    )
    return jax.shard_map(
        local,
        mesh=wide,
        in_specs=placed,
        out_specs=(P(seq, mp), P(seq, mp)),
        check_vma=False,
    )
```

```python
import functools

import jax
import jax.numpy as jnp
from jax import lax
from jax.experimental import pallas as pl
from jax.experimental.pallas import tpu as pltpu
from jax.sharding import Mesh, PartitionSpec as P

AXES = ("z", "y", "x", "c")
SHORT_CALL = pl.CostEstimate(flops=1, bytes_accessed=1, transcendentals=0)


def factors(mesh):
    seq, mp = mesh.shape["seq"], mesh.shape["mp"]
    along_y = 1
    while 2 * along_y * along_y < seq:
        along_y *= 2
    return seq // along_y, along_y, mp // 2, 2


def rotate(value, axis, by):
    size = lax.axis_size(axis)
    return lax.ppermute(value, axis, [(i, (i + by) % size) for i in range(size)])


def blank_kernel(out_ref):
    del out_ref


def blank(shape, dtype):
    return pl.pallas_call(
        blank_kernel, out_specs=pl.BlockSpec(memory_space=pl.ANY), out_shape=jax.ShapeDtypeStruct(shape, dtype)
    )()


class Steps:
    def __init__(self):
        self.gate, self.open = (), []

    def __call__(self, send, value, *earlier, wait=True):
        found = send(after(value, *self.gate, *earlier))
        if wait:
            self.open.append(found)
        return found

    def then(self, *others):
        self.gate, self.open = tuple(self.open) + others, []


def after(value, *earlier):
    return lax.optimization_barrier((value, *earlier))[0]


def split_kernel(source, gain, target):
    target[0] = (source[0, 0].astype(jnp.float32) * gain[...]).astype(jnp.bfloat16)


def split_weights(in_weight, block, c, gain):
    parts = lax.axis_size("z")
    rows, columns = in_weight.shape[2], in_weight.shape[3] // parts
    if columns % 128:
        scaled = (in_weight[block, c].astype(jnp.float32) * gain).astype(jnp.bfloat16)
        return scaled.reshape(rows, parts, columns).transpose(1, 0, 2)
    return pl.pallas_call(
        split_kernel,
        grid=(parts,),
        in_specs=[
            pl.BlockSpec((1, 1, rows, columns), lambda k: (block, c, 0, k)),
            pl.BlockSpec((rows, 1), lambda k: (0, 0)),
        ],
        out_specs=pl.BlockSpec((1, rows, columns), lambda k: (k, 0, 0)),
        cost_estimate=SHORT_CALL,
        out_shape=jax.ShapeDtypeStruct((parts, rows, columns), jnp.bfloat16),
    )(in_weight, gain)


def exchange(pieces):
    return lax.all_to_all(pieces, "z", 0, 0, tiled=True)


def others(axis, value, send):
    moves = [functools.partial(rotate, axis=axis, by=j) for j in range(1, lax.axis_size(axis))]
    return [value] + [send(move, value) for move in moves]


def at_once(move, value):
    return move(value)


def slot_of(z_from, x_at, c_at):
    x_size, c_size = lax.axis_size("x"), lax.axis_size("c")
    x_from, c_from = z_from // c_size, z_from % c_size
    return ((x_at - x_from) % x_size) * c_size + (c_at - c_from) % c_size


def placed_rows(found, places, where):
    _, y_at, x_at, c_at = where
    parts, y_size = lax.axis_size("z"), lax.axis_size("y")
    rows, columns = found[0][0].shape
    whole = blank((parts, y_size, rows, columns), found[0][0].dtype)
    for group, place in zip(found, places):
        slot = slot_of(place, x_at, c_at)
        for j, piece in enumerate(group):
            whole = lax.dynamic_update_slice(whole, piece[None, None], (slot, (y_at - j) % y_size, 0, 0))
    return whole.reshape(parts * y_size * rows, columns)


def all_of_c(found):
    return [rotate(p, "c", d) if d else p for p in found for d in range(lax.axis_size("c"))]


def next_along_z(value):
    return rotate(value, "z", 1)


def project_kernel(groups, order_ref, *refs):
    count = len(refs) - 5
    pieces = refs[: count - 3 * (order_ref.shape[0] - groups[1])]
    weights = refs[len(pieces) : count]
    out_ref, held, total, squares, arrived = refs[-5:]
    step = pl.program_id(0)
    y_size = len(weights) // 3
    deep, width = weights[0].shape[1], weights[0].shape[2]
    rows = pieces[0].shape[0]

    def arrival(g, r):
        return pltpu.make_async_copy(
            pieces[g * groups[1] + r], held.at[r, pl.ds(g * rows, rows)], arrived.at[r, g]
        )

    @pl.when(step == 0)
    def _():
        for r in range(groups[1]):
            for g in range(groups[0]):
                arrival(g, r).start()
        total[...] = jnp.zeros_like(total)
        squares[...] = jnp.zeros_like(squares)

    for r in range(groups[1]):

        @pl.when(step == r)
        def _(r=r):
            for g in range(groups[0]):
                arrival(g, r).wait()

    for g in range(groups[0]):
        these = slice(g * rows, (g + 1) * rows)
        values = held[step, these].astype(jnp.float32)
        squares[these] += jnp.sum(values * values, axis=1, keepdims=True)
    for c in range(3):
        some = 0.0
        for j in range(y_size):
            begin = pl.multiple_of(order_ref[groups[1] + j] * deep, deep)
            some = some + jnp.dot(
                held[step, :, pl.ds(begin, deep)], weights[c * y_size + j][0], preferred_element_type=jnp.float32
            )
        total[:, c * width : (c + 1) * width] += some

    @pl.when(step == groups[1] - 1)
    def _():
        scale = lax.rsqrt(squares[...] / (groups[1] * pieces[0].shape[1]) + 1e-06)
        out_ref[...] = (total[...] * scale).astype(out_ref.dtype)


def project(found, weights, order):
    groups = (len(found), len(found[0]))
    flat = [w for group in weights for w in group]
    pieces = [p for group in found for p in group]
    rows, features_here = pieces[0].shape
    width = flat[0].shape[2]
    out = pl.pallas_call(
        functools.partial(project_kernel, groups),
        grid_spec=pltpu.PrefetchScalarGridSpec(
            num_scalar_prefetch=1,
            grid=(groups[1],),
            in_specs=[pl.BlockSpec(memory_space=pl.ANY)] * len(pieces)
            + [pl.BlockSpec((1,) + w.shape[1:], lambda r, order: (order[r], 0, 0)) for w in flat],
            out_specs=pl.BlockSpec((groups[0] * rows, 3 * width), lambda r, order: (0, 0)),
            scratch_shapes=[
                pltpu.VMEM((groups[1], groups[0] * rows, features_here), jnp.bfloat16),
                pltpu.VMEM((groups[0] * rows, 3 * width), jnp.float32),
                pltpu.VMEM((groups[0] * rows, 1), jnp.float32),
                pltpu.SemaphoreType.DMA((groups[1], groups[0])),
            ],
        ),
        out_shape=jax.ShapeDtypeStruct((groups[0] * rows, 3 * width), jnp.bfloat16),
        compiler_params=pltpu.CompilerParams(vmem_limit_bytes=48 * 2**20),
    )(order, *pieces, *flat)
    return out.reshape(groups[0], rows, 3 * width)


def mix_table(z_at, y_at, places):
    parts = len(places)
    stacked = jnp.stack(places)
    behind = jnp.where(y_at == 0, stacked[(stacked - 1) % parts], jnp.arange(parts))
    some = jnp.where((y_at == 0) & (stacked == 0), 0, 1)
    return jnp.stack([behind, some, stacked]).astype(jnp.int32)


def delayed(value, by):
    return pltpu.roll(value, by, 0) if by else value


def taps_sum(value, taps):
    total = taps[0] * value
    for s in range(1, len(taps)):
        total = total + taps[s] * delayed(value, s)
    return total


def features(lanes, width, start, table_ref, proj_ref, before_ref, feat_ref):
    some = table_ref[1, pl.program_id(0)].astype(jnp.float32)
    out = []
    for c in range(3):
        begin = c * width + start
        before = before_ref[0, :, begin : begin + lanes].astype(jnp.float32) * some
        value = jnp.concatenate([before, proj_ref[0, :, begin : begin + lanes].astype(jnp.float32)], axis=0)
        taps = [feat_ref[c, s : s + 1, start : start + lanes] for s in range(feat_ref.shape[1])]
        out.append(taps_sum(value, taps))
    return out


def short_kernel(table_ref, proj_ref, before_ref, feat_ref, taps_ref, out_ref):
    width = out_ref.shape[2]
    lanes = min(128, width)
    rim = before_ref.shape[1]
    for start in range(0, width, lanes):
        query, key, value = features(lanes, width, start, table_ref, proj_ref, before_ref, feat_ref)
        kv = (key * value).astype(jnp.bfloat16).astype(jnp.float32)
        taps = [taps_ref[s : s + 1, start : start + lanes] for s in range(taps_ref.shape[0])]
        inner = taps_sum(kv, taps)
        out_ref[0, :, start : start + lanes] = (query[rim:] * inner[rim:]).astype(out_ref.dtype)


def gate_kernel(table_ref, proj_ref, before_ref, feat_ref, query_ref, kv_ref):
    width = kv_ref.shape[2]
    lanes = min(128, width)
    rim = before_ref.shape[1]
    for start in range(0, width, lanes):
        query, key, value = features(lanes, width, start, table_ref, proj_ref, before_ref, feat_ref)
        query_ref[0, :, start : start + lanes] = query[rim:]
        kv_ref[0, :, start : start + lanes] = (key[rim:] * value[rim:]).astype(kv_ref.dtype)


def medium_kernel(table_ref, query_ref, kv_ref, before_ref, matrix_ref, out_ref):
    groups, span = matrix_ref.shape[0], matrix_ref.shape[1]
    count, width = out_ref.shape[1], out_ref.shape[2]
    lanes = min(128, width)
    per_group = width // groups
    some = table_ref[1, pl.program_id(0)]
    before = before_ref[0]
    before = jnp.where(some > 0, before, jnp.zeros_like(before))
    lane = lax.broadcasted_iota(jnp.int32, (span, lanes), 1) // per_group
    for block in range(count // span):
        own = kv_ref[0, block * span : (block + 1) * span]
        pair = jnp.concatenate([before, own], axis=0)
        before = own
        rows = slice(block * span, (block + 1) * span)
        for start in range(0, width, lanes):
            inner = jnp.zeros((span, lanes), jnp.float32)
            for g in range(lanes // per_group):
                taken = jnp.dot(
                    matrix_ref[start // per_group + g], pair[:, start : start + lanes], preferred_element_type=jnp.float32
                )
                inner = jnp.where(lane == g, taken, inner)
            query = query_ref[0, rows, start : start + lanes]
            out_ref[0, rows, start : start + lanes] = (query * inner).astype(out_ref.dtype)


def whole_spec(value):
    return pl.BlockSpec(value.shape, lambda i, table: (0,) * value.ndim)


def piece_spec(value, which=None):
    def index(i, table):
        return (i if which is None else table[which, i], 0, 0)

    return pl.BlockSpec((1,) + value.shape[1:], index)


def short_mix(proj, feat, taps, table):
    before = rotate(proj[:, proj.shape[1] - 16 :], "y", 1)
    out = jax.ShapeDtypeStruct(proj.shape[:2] + (proj.shape[2] // 3,), jnp.bfloat16)
    return pl.pallas_call(
        short_kernel,
        grid_spec=pltpu.PrefetchScalarGridSpec(
            num_scalar_prefetch=1,
            grid=(proj.shape[0],),
            in_specs=[piece_spec(proj), piece_spec(before, 0), whole_spec(feat), whole_spec(taps)],
            out_specs=piece_spec(out, 2),
        ),
        cost_estimate=SHORT_CALL,
        out_shape=out,
    )(table, proj, before, feat, taps)


def medium_mix(proj, feat, matrix, table):
    before = rotate(proj[:, proj.shape[1] - 16 :], "y", 1)
    shape = proj.shape[:2] + (proj.shape[2] // 3,)
    query = jax.ShapeDtypeStruct(shape, jnp.float32)
    kv = jax.ShapeDtypeStruct(shape, jnp.bfloat16)
    query, kv = pl.pallas_call(
        gate_kernel,
        grid_spec=pltpu.PrefetchScalarGridSpec(
            num_scalar_prefetch=1,
            grid=(proj.shape[0],),
            in_specs=[piece_spec(proj), piece_spec(before, 0), whole_spec(feat)],
            out_specs=[piece_spec(query), piece_spec(kv)],
        ),
        cost_estimate=SHORT_CALL,
        out_shape=[query, kv],
    )(table, proj, before, feat)
    before = rotate(kv[:, kv.shape[1] - matrix.shape[1] :], "y", 1)
    return pl.pallas_call(
        medium_kernel,
        grid_spec=pltpu.PrefetchScalarGridSpec(
            num_scalar_prefetch=1,
            grid=(proj.shape[0],),
            in_specs=[piece_spec(query), piece_spec(kv), piece_spec(before, 0), whole_spec(matrix)],
            out_specs=piece_spec(kv, 2),
        ),
        cost_estimate=SHORT_CALL,
        out_shape=jax.ShapeDtypeStruct(shape, jnp.bfloat16),
    )(table, query, kv, before, matrix)


def toeplitz_kernel(row_ref, out_ref):
    width = out_ref.shape[1]
    rows = jnp.broadcast_to(row_ref[0], (width, 3 * width))
    turned = pltpu.roll(rows, 0, 1, stride=1, stride_axis=0)
    out_ref[0] = turned[:, : 2 * width].astype(out_ref.dtype)


def toeplitz(filt):
    groups, width = filt.shape
    row = jnp.concatenate([jnp.zeros((groups, 1)), filt[:, ::-1], jnp.zeros((groups, 2 * width - 1))], axis=1)[:, None]
    return pl.pallas_call(
        toeplitz_kernel,
        grid=(groups,),
        in_specs=[pl.BlockSpec((1, 1, 3 * width), lambda g: (g, 0, 0))],
        out_specs=pl.BlockSpec((1, width, 2 * width), lambda g: (g, 0, 0)),
        cost_estimate=SHORT_CALL,
        out_shape=jax.ShapeDtypeStruct((groups, width, 2 * width), jnp.bfloat16),
    )(row)


def channels_of(value, z_at, axis):
    size = value.shape[axis] // lax.axis_size("z")
    return lax.dynamic_slice_in_dim(value, z_at * size, size, axis)


def home(pieces):
    back = exchange(pieces)
    return jnp.concatenate([back[k] for k in range(back.shape[0])], axis=1)


def local(tokens, norm_gain, in_weight, feat_filter, short_filter, medium_filter, out_weight):
    where = tuple(lax.axis_index(a) for a in AXES)
    z_at, y_at, x_at, c_at = where
    parts = lax.axis_size("z")
    rows = in_weight.shape[2]
    width = in_weight.shape[3] // parts
    begin = (z_at * lax.axis_size("y") + y_at) * rows
    gains = lax.dynamic_slice_in_dim(norm_gain, begin, rows, 1)[:, :, None]
    feat = channels_of(feat_filter, z_at, 3)
    short = channels_of(short_filter, z_at, 0)
    short_taps = jnp.repeat(short.T, width // short.shape[0], axis=1)
    matrix = toeplitz(channels_of(medium_filter, z_at, 0))
    places = [(z_at - k) % parts for k in range(parts)]
    table = mix_table(z_at, y_at, places)
    x_size, c_size, y_size = (lax.axis_size(a) for a in ("x", "c", "y"))
    order = [((x_at - d) % x_size) * c_size + (c_at - e) % c_size for d in range(x_size) for e in range(c_size)]
    order = jnp.stack(order + [(y_at - j) % y_size for j in range(y_size)]).astype(jnp.int32)

    def split(block, c):
        return split_weights(in_weight, block, c, gains[block])

    step = Steps()
    ring, found, came, weights = [tokens], [], [], []
    rows_ring, held = [out_weight], []
    for k in range(parts):
        if k < parts - 1:
            ring.append(step(next_along_z, ring[k]))
        else:
            rows_ring.append(step(next_along_z, out_weight))
        if k < 3:
            came.append(step(exchange, split(0, k)))
        found.append(others("x", ring[k], step))
        if k == 0:
            held.append(others("y", out_weight, step))
        elif k <= 3:
            weights.append(others("y", came[k - 1], step))
        step.then(*([matrix] if k == 1 else []))
    proj = project([all_of_c(group) for group in found], weights, order)
    gated = short_mix(proj, feat[0], short_taps, table)
    back = home(gated)
    for k in range(1, parts):
        if k < parts - 1:
            rows_ring.append(step(next_along_z, rows_ring[k]))
            held.append(others("y", rows_ring[k], step))
            step.then()
    held.append(others("y", rows_ring[-1], step))
    came, weights_next = [], []
    for k in range(4):
        if k < 3:
            came.append(step(exchange, split(1, k), back))
        if k:
            weights_next.append(others("y", came[k - 1], step))
        step.then()
    first = jnp.concatenate(all_of_c(others("x", back, at_once)), axis=1)
    out_rows = placed_rows(held, places, where)
    delta = jnp.dot(first, out_rows, preferred_element_type=jnp.float32)
    stream = (tokens.astype(jnp.float32) + delta).astype(jnp.bfloat16)

    step = Steps()
    ring, found = [stream], []
    for k in range(parts):
        if k < parts - 1:
            ring.append(step(next_along_z, ring[k]))
        found.append(others("x", ring[k], step))
        step.then()
    found = [all_of_c(group) for group in found[:-1]] + [found[-1]]
    proj = [project(found[:2], weights_next, order)]
    for group in found[2:-1]:
        proj.append(project([group], weights_next, order))
    last = found[-1][:1] + [after(p, *proj) for p in found[-1][1:]]
    proj.append(project([all_of_c(last)], weights_next, order))
    gated = medium_mix(jnp.concatenate(proj), feat[1], matrix, table)
    return stream, home(gated)


def solution(mesh):
    wide = Mesh(mesh.devices.reshape(factors(mesh)), AXES)
    seq, mp = ("z", "y"), ("x", "c")
    placed = (
        P(seq, mp),
        P(),
        P(None, None, seq, mp),
        P(None, None, None, mp),
        P(mp, None),
        P(mp, None),
        P(seq, mp),
    )
    return jax.shard_map(
        local,
        mesh=wide,
        in_specs=placed,
        out_specs=(P(seq, mp), P(seq, mp)),
        check_vma=False,
    )
```

```python
import functools

import jax
import jax.numpy as jnp
from jax import lax
from jax.experimental import pallas as pl
from jax.experimental.pallas import tpu as pltpu
from jax.sharding import Mesh, PartitionSpec as P

AXES = ("z", "y", "x", "c")
MIB = 2**20
SHORT_CALL = pl.CostEstimate(flops=1, bytes_accessed=1, transcendentals=0)
SMALL = pltpu.CompilerParams(vmem_limit_bytes=10 * MIB)


def factors(mesh):
    seq, mp = mesh.shape["seq"], mesh.shape["mp"]
    along_y = 1
    while 2 * along_y * along_y < seq:
        along_y *= 2
    return seq // along_y, along_y, mp // 2, 2


def rotate(value, axis, by):
    size = lax.axis_size(axis)
    return lax.ppermute(value, axis, [(i, (i + by) % size) for i in range(size)])


class Steps:
    def __init__(self):
        self.gate, self.open = (), []

    def __call__(self, send, value, *earlier, wait=True):
        found = send(after(value, *self.gate, *earlier))
        if wait:
            self.open.append(found)
        return found

    def then(self, *others):
        self.gate, self.open = tuple(self.open) + others, []


def after(value, *earlier):
    return lax.optimization_barrier((value, *earlier))[0]


def split_kernel(source, gain, target):
    target[0] = (source[0, 0].astype(jnp.float32) * gain[...]).astype(jnp.bfloat16)


def split_weights(in_weight, block, c, gain):
    parts = lax.axis_size("z")
    rows, columns = in_weight.shape[2], in_weight.shape[3] // parts
    if columns % 128:
        scaled = (in_weight[block, c].astype(jnp.float32) * gain).astype(jnp.bfloat16)
        return scaled.reshape(rows, parts, columns).transpose(1, 0, 2)
    return pl.pallas_call(
        split_kernel,
        grid=(parts,),
        in_specs=[
            pl.BlockSpec((1, 1, rows, columns), lambda k: (block, c, 0, k)),
            pl.BlockSpec((rows, 1), lambda k: (0, 0)),
        ],
        out_specs=pl.BlockSpec((1, rows, columns), lambda k: (k, 0, 0)),
        cost_estimate=SHORT_CALL,
        compiler_params=SMALL,
        out_shape=jax.ShapeDtypeStruct((parts, rows, columns), jnp.bfloat16),
    )(in_weight, gain)


def exchange(pieces):
    return lax.all_to_all(pieces, "z", 0, 0, tiled=True)


def others(axis, value, send):
    moves = [functools.partial(rotate, axis=axis, by=j) for j in range(1, lax.axis_size(axis))]
    return [value] + [send(move, value) for move in moves]


def at_once(move, value):
    return move(value)


def slot_of(z_from, x_at, c_at):
    x_size, c_size = lax.axis_size("x"), lax.axis_size("c")
    x_from, c_from = z_from // c_size, z_from % c_size
    return ((x_at - x_from) % x_size) * c_size + (c_at - c_from) % c_size


def joined_kernel(blocks, place_ref, tokens_ref, *refs):
    firsts, rows = refs[:blocks], refs[blocks:-5]
    out_ref, first_held, rows_held, first_came, rows_came = refs[-5:]
    parts = place_ref.shape[0] // 2
    y_size = len(rows) // parts
    deep = rows[0].shape[0]

    def first_arrival(r):
        return pltpu.make_async_copy(firsts[r], first_held.at[r], first_came.at[r])

    def rows_arrival(n):
        return pltpu.make_async_copy(rows[n], rows_held.at[n], rows_came.at[n])

    for r in range(blocks):
        first_arrival(r).start()
    for n in range(len(rows)):
        rows_arrival(n).start()
    for r in range(blocks):
        first_arrival(r).wait()
    total = tokens_ref[...].astype(jnp.float32)
    for n in range(len(rows)):
        rows_arrival(n).wait()
        begin = pl.multiple_of(place_ref[parts + n % y_size] * deep, deep)
        total = total + jnp.dot(
            first_held[place_ref[n // y_size], :, pl.ds(begin, deep)], rows_held[n], preferred_element_type=jnp.float32
        )
    out_ref[...] = total.astype(out_ref.dtype)


def joined(tokens, first, held, places, where):
    _, y_at, x_at, c_at = where
    parts, y_size = len(held), len(held[0])
    place = [slot_of(p, x_at, c_at) for p in places] + [(y_at - j) % y_size for j in range(y_size)]
    place += [y_at * 0] * (2 * parts - len(place))
    rows = [w for group in held for w in group]
    anywhere = pl.BlockSpec(memory_space=pl.ANY)
    return pl.pallas_call(
        functools.partial(joined_kernel, len(first)),
        grid_spec=pltpu.PrefetchScalarGridSpec(
            num_scalar_prefetch=1,
            grid=(1,),
            in_specs=[pl.BlockSpec(tokens.shape, lambda i, place: (0, 0))] + [anywhere] * (len(first) + len(rows)),
            out_specs=pl.BlockSpec(tokens.shape, lambda i, place: (0, 0)),
            scratch_shapes=[
                pltpu.VMEM((len(first),) + first[0].shape, jnp.bfloat16),
                pltpu.VMEM((len(rows),) + rows[0].shape, jnp.bfloat16),
                pltpu.SemaphoreType.DMA((len(first),)),
                pltpu.SemaphoreType.DMA((len(rows),)),
            ],
        ),
        out_shape=jax.ShapeDtypeStruct(tokens.shape, tokens.dtype),
        compiler_params=pltpu.CompilerParams(vmem_limit_bytes=48 * 2**20),
    )(jnp.stack(place).astype(jnp.int32), tokens, *first, *rows)


def all_of_c(found):
    return [rotate(p, "c", d) if d else p for p in found for d in range(lax.axis_size("c"))]


def next_along_z(value):
    return rotate(value, "z", 1)


def project_kernel(groups, order_ref, *refs):
    count = len(refs) - 5
    pieces = refs[: count - 3 * (order_ref.shape[0] - groups[1])]
    weights = refs[len(pieces) : count]
    out_ref, held, total, squares, arrived = refs[-5:]
    step = pl.program_id(0)
    y_size = len(weights) // 3
    deep, width = weights[0].shape[1], weights[0].shape[2]
    rows = pieces[0].shape[0]

    def arrival(g, r):
        return pltpu.make_async_copy(
            pieces[g * groups[1] + r], held.at[r, pl.ds(g * rows, rows)], arrived.at[r, g]
        )

    @pl.when(step == 0)
    def _():
        for r in range(groups[1]):
            for g in range(groups[0]):
                arrival(g, r).start()
        total[...] = jnp.zeros_like(total)
        squares[...] = jnp.zeros_like(squares)

    for r in range(groups[1]):

        @pl.when(step == r)
        def _(r=r):
            for g in range(groups[0]):
                arrival(g, r).wait()

    for g in range(groups[0]):
        these = slice(g * rows, (g + 1) * rows)
        values = held[step, these].astype(jnp.float32)
        squares[these] += jnp.sum(values * values, axis=1, keepdims=True)
    for c in range(3):
        some = 0.0
        for j in range(y_size):
            begin = pl.multiple_of(order_ref[groups[1] + j] * deep, deep)
            some = some + jnp.dot(
                held[step, :, pl.ds(begin, deep)], weights[c * y_size + j][0], preferred_element_type=jnp.float32
            )
        total[:, c * width : (c + 1) * width] += some

    @pl.when(step == groups[1] - 1)
    def _():
        scale = lax.rsqrt(squares[...] / (groups[1] * pieces[0].shape[1]) + 1e-06)
        out_ref[...] = (total[...] * scale).astype(out_ref.dtype)


def project(found, weights, order):
    groups = (len(found), len(found[0]))
    flat = [w for group in weights for w in group]
    pieces = [p for group in found for p in group]
    rows, features_here = pieces[0].shape
    width = flat[0].shape[2]
    needed = groups[0] * rows * (groups[1] * features_here * 2 + 3 * width * 8 + 512) + 12 * flat[0][0].size * len(flat) // 3
    out = pl.pallas_call(
        functools.partial(project_kernel, groups),
        grid_spec=pltpu.PrefetchScalarGridSpec(
            num_scalar_prefetch=1,
            grid=(groups[1],),
            in_specs=[pl.BlockSpec(memory_space=pl.ANY)] * len(pieces)
            + [pl.BlockSpec((1,) + w.shape[1:], lambda r, order: (order[r], 0, 0)) for w in flat],
            out_specs=pl.BlockSpec((groups[0] * rows, 3 * width), lambda r, order: (0, 0)),
            scratch_shapes=[
                pltpu.VMEM((groups[1], groups[0] * rows, features_here), jnp.bfloat16),
                pltpu.VMEM((groups[0] * rows, 3 * width), jnp.float32),
                pltpu.VMEM((groups[0] * rows, 1), jnp.float32),
                pltpu.SemaphoreType.DMA((groups[1], groups[0])),
            ],
        ),
        out_shape=jax.ShapeDtypeStruct((groups[0] * rows, 3 * width), jnp.bfloat16),
        compiler_params=pltpu.CompilerParams(vmem_limit_bytes=48 * 2**20),
    )(order, *pieces, *flat)
    return out.reshape(groups[0], rows, 3 * width)


def mix_table(z_at, y_at, places):
    parts = len(places)
    stacked = jnp.stack(places)
    behind = jnp.where(y_at == 0, stacked[(stacked - 1) % parts], jnp.arange(parts))
    some = jnp.where((y_at == 0) & (stacked == 0), 0, 1)
    return jnp.stack([behind, some, stacked]).astype(jnp.int32)


def delayed(value, by):
    return pltpu.roll(value, by, 0) if by else value


def taps_sum(value, taps):
    total = taps[0] * value
    for s in range(1, len(taps)):
        total = total + taps[s] * delayed(value, s)
    return total


def features(lanes, width, start, table_ref, proj_ref, before_ref, feat_ref):
    some = table_ref[1, pl.program_id(0)].astype(jnp.float32)
    out = []
    for c in range(3):
        begin = c * width + start
        before = before_ref[0, :, begin : begin + lanes].astype(jnp.float32) * some
        value = jnp.concatenate([before, proj_ref[0, :, begin : begin + lanes].astype(jnp.float32)], axis=0)
        taps = [feat_ref[c, s : s + 1, start : start + lanes] for s in range(feat_ref.shape[1])]
        out.append(taps_sum(value, taps))
    return out


def short_kernel(table_ref, proj_ref, before_ref, feat_ref, taps_ref, out_ref):
    width = out_ref.shape[2]
    lanes = min(128, width)
    rim = before_ref.shape[1]
    for start in range(0, width, lanes):
        query, key, value = features(lanes, width, start, table_ref, proj_ref, before_ref, feat_ref)
        kv = (key * value).astype(jnp.bfloat16).astype(jnp.float32)
        taps = [taps_ref[s : s + 1, start : start + lanes] for s in range(taps_ref.shape[0])]
        inner = taps_sum(kv, taps)
        out_ref[0, :, start : start + lanes] = (query[rim:] * inner[rim:]).astype(out_ref.dtype)


def gate_kernel(table_ref, proj_ref, before_ref, feat_ref, query_ref, kv_ref):
    width = kv_ref.shape[2]
    lanes = min(128, width)
    rim = before_ref.shape[1]
    for start in range(0, width, lanes):
        query, key, value = features(lanes, width, start, table_ref, proj_ref, before_ref, feat_ref)
        query_ref[0, :, start : start + lanes] = query[rim:]
        kv_ref[0, :, start : start + lanes] = (key[rim:] * value[rim:]).astype(kv_ref.dtype)


def medium_kernel(table_ref, query_ref, kv_ref, before_ref, matrix_ref, out_ref):
    groups, span = matrix_ref.shape[0], matrix_ref.shape[1]
    count, width = out_ref.shape[1], out_ref.shape[2]
    lanes = min(128, width)
    per_group = width // groups
    some = table_ref[1, pl.program_id(0)]
    before = before_ref[0]
    before = jnp.where(some > 0, before, jnp.zeros_like(before))
    lane = lax.broadcasted_iota(jnp.int32, (span, lanes), 1) // per_group
    for block in range(count // span):
        own = kv_ref[0, block * span : (block + 1) * span]
        pair = jnp.concatenate([before, own], axis=0)
        before = own
        rows = slice(block * span, (block + 1) * span)
        for start in range(0, width, lanes):
            inner = jnp.zeros((span, lanes), jnp.float32)
            for g in range(lanes // per_group):
                taken = jnp.dot(
                    matrix_ref[start // per_group + g], pair[:, start : start + lanes], preferred_element_type=jnp.float32
                )
                inner = jnp.where(lane == g, taken, inner)
            query = query_ref[0, rows, start : start + lanes]
            out_ref[0, rows, start : start + lanes] = (query * inner).astype(out_ref.dtype)


def whole_spec(value):
    return pl.BlockSpec(value.shape, lambda i, table: (0,) * value.ndim)


def piece_spec(value, which=None):
    def index(i, table):
        return (i if which is None else table[which, i], 0, 0)

    return pl.BlockSpec((1,) + value.shape[1:], index)


def tails(pieces, count):
    return rotate(pieces[:, pieces.shape[1] - count :], "y", 1)


def short_mix(proj, before, feat, taps, table):
    out = jax.ShapeDtypeStruct(proj.shape[:2] + (proj.shape[2] // 3,), jnp.bfloat16)
    return pl.pallas_call(
        short_kernel,
        grid_spec=pltpu.PrefetchScalarGridSpec(
            num_scalar_prefetch=1,
            grid=(proj.shape[0],),
            in_specs=[piece_spec(proj), piece_spec(before, 0), whole_spec(feat), whole_spec(taps)],
            out_specs=piece_spec(out, 2),
        ),
        cost_estimate=SHORT_CALL,
        compiler_params=SMALL,
        out_shape=out,
    )(table, proj, before, feat, taps)


def medium_mix(proj, feat, matrix, table, z_at):
    before = tails(proj, 16)
    shape = proj.shape[:2] + (proj.shape[2] // 3,)
    query = jax.ShapeDtypeStruct(shape, jnp.float32)
    kv = jax.ShapeDtypeStruct(shape, jnp.bfloat16)
    query, kv = pl.pallas_call(
        gate_kernel,
        grid_spec=pltpu.PrefetchScalarGridSpec(
            num_scalar_prefetch=1,
            grid=(proj.shape[0],),
            in_specs=[piece_spec(proj), piece_spec(before, 0), whole_spec(feat)],
            out_specs=[piece_spec(query), piece_spec(kv)],
        ),
        cost_estimate=SHORT_CALL,
        compiler_params=SMALL,
        out_shape=[query, kv],
    )(table, proj, before, feat)
    before = tails(kv, matrix.shape[1])
    parts = proj.shape[0]
    far = medium(query, kv, before, matrix, table, range(parts // 2, parts))
    close = medium(query, kv, before, matrix, table, range(parts // 2))
    made = [close[k] for k in range(parts // 2)] + [far[k] for k in range(parts - parts // 2)]
    back = [rotate(piece, "z", -k) if k else piece for k, piece in enumerate(made)]
    stacked = jnp.stack(back)
    ordered = [lax.dynamic_index_in_dim(stacked, (k - z_at) % parts, 0, keepdims=False) for k in range(parts)]
    return jnp.concatenate(ordered, axis=1)


def medium(query, kv, before, matrix, table, which):
    count = len(which)
    table = jnp.concatenate([table[:, which.start : which.stop], jnp.arange(which.start, which.stop, dtype=jnp.int32)[None]])
    shape = (count,) + kv.shape[1:]
    return pl.pallas_call(
        medium_kernel,
        grid_spec=pltpu.PrefetchScalarGridSpec(
            num_scalar_prefetch=1,
            grid=(count,),
            in_specs=[piece_spec(query, 3), piece_spec(kv, 3), piece_spec(before, 0), whole_spec(matrix)],
            out_specs=piece_spec(kv),
        ),
        cost_estimate=SHORT_CALL,
        compiler_params=SMALL,
        out_shape=jax.ShapeDtypeStruct(shape, jnp.bfloat16),
    )(table, query, kv, before, matrix)


def toeplitz_kernel(row_ref, out_ref):
    width = out_ref.shape[1]
    rows = jnp.broadcast_to(row_ref[0], (width, 3 * width))
    turned = pltpu.roll(rows, 0, 1, stride=1, stride_axis=0)
    out_ref[0] = turned[:, : 2 * width].astype(out_ref.dtype)


def toeplitz(filt):
    groups, width = filt.shape
    row = jnp.concatenate([jnp.zeros((groups, 1)), filt[:, ::-1], jnp.zeros((groups, 2 * width - 1))], axis=1)[:, None]
    return pl.pallas_call(
        toeplitz_kernel,
        grid=(groups,),
        in_specs=[pl.BlockSpec((1, 1, 3 * width), lambda g: (g, 0, 0))],
        out_specs=pl.BlockSpec((1, width, 2 * width), lambda g: (g, 0, 0)),
        cost_estimate=SHORT_CALL,
        compiler_params=SMALL,
        out_shape=jax.ShapeDtypeStruct((groups, width, 2 * width), jnp.bfloat16),
    )(row)


def channels_of(value, z_at, axis):
    size = value.shape[axis] // lax.axis_size("z")
    return lax.dynamic_slice_in_dim(value, z_at * size, size, axis)


def home(pieces):
    back = exchange(pieces)
    return jnp.concatenate([back[k] for k in range(back.shape[0])], axis=1)


def local(tokens, norm_gain, in_weight, feat_filter, short_filter, medium_filter, out_weight):
    where = tuple(lax.axis_index(a) for a in AXES)
    z_at, y_at, x_at, c_at = where
    parts = lax.axis_size("z")
    rows = in_weight.shape[2]
    width = in_weight.shape[3] // parts
    begin = (z_at * lax.axis_size("y") + y_at) * rows
    gains = lax.dynamic_slice_in_dim(norm_gain, begin, rows, 1)[:, :, None]
    feat = channels_of(feat_filter, z_at, 3)
    short = channels_of(short_filter, z_at, 0)
    short_taps = jnp.repeat(short.T, width // short.shape[0], axis=1)
    matrix = toeplitz(channels_of(medium_filter, z_at, 0))
    places = [(z_at - k) % parts for k in range(parts)]
    table = mix_table(z_at, y_at, places)
    x_size, c_size, y_size = (lax.axis_size(a) for a in ("x", "c", "y"))
    order = [((x_at - d) % x_size) * c_size + (c_at - e) % c_size for d in range(x_size) for e in range(c_size)]
    order = jnp.stack(order + [(y_at - j) % y_size for j in range(y_size)]).astype(jnp.int32)

    def split(block, c):
        return split_weights(in_weight, block, c, gains[block])

    step = Steps()
    ring, found, came, weights = [tokens], [], [], []
    rows_ring, held = [out_weight], []
    splits = [split(1, c) for c in range(3)]
    for k in range(parts):
        if k < parts - 1:
            ring.append(step(next_along_z, ring[k]))
        else:
            rows_ring.append(step(next_along_z, out_weight))
        if k < 3:
            came.append(step(exchange, split(0, k)))
        found.append([others("c", ring[k], step)])
        fresh = others("x", ring[k], step)[1:]
        if k:
            found[k - 1] += [others("c", piece, step) for piece in waiting]
        waiting = fresh
        if k == 0:
            held.append(others("y", out_weight, step))
        elif k <= 3:
            weights.append(others("y", came[k - 1], step))
        step.then(*([matrix] if k == 1 else splits if k == 2 else []))
    found[-1] += [others("c", piece, at_once) for piece in waiting]
    proj = project([sum(group, []) for group in found], weights, order)
    near = tails(after(proj, *step.gate), 16)
    for k in range(1, parts - 1):
        rows_ring.append(step(next_along_z, rows_ring[k]))
        held.append(others("y", after(rows_ring[k], near) if k == parts - 2 else rows_ring[k], step))
        step.then(proj)
    gated = short_mix(proj, near, feat[0], short_taps, table)
    back = home(after(gated, rows_ring[-1], *held[-1]))
    held.append(others("y", after(rows_ring[-1], *held[-1]), at_once))
    first = all_of_c(others("x", after(back, *held[-1]), at_once))
    step.then(*step.gate, back)
    came, weights_next = [step(exchange, splits[0])], []
    came.append(exchange(after(splits[1], came[0], *first)))
    stream = joined(tokens, first, held, places, where)

    step.then(stream)
    ring, found = [stream], []
    for k in range(parts):
        if k < parts - 1:
            ring.append(step(next_along_z, ring[k]))
        if k == 1:
            came.append(step(exchange, splits[2]))
        found.append([others("c", ring[k], step)])
        fresh = others("x", ring[k], step)[1:]
        if k:
            found[k - 1] += [others("c", piece, step) for piece in waiting]
        waiting = fresh
        if k < 3:
            weights_next.append(others("y", came[k], step))
        step.then()
    early = [sum(group, []) for group in found[:-1]]
    proj = [project(early, weights_next, order)]
    found[-1] += [others("c", after(piece, *proj), at_once) for piece in waiting]
    proj.append(project([sum(found[-1], [])], weights_next, order))
    return stream, medium_mix(jnp.concatenate(proj), feat[1], matrix, table, z_at)


def solution(mesh):
    wide = Mesh(mesh.devices.reshape(factors(mesh)), AXES)
    seq, mp = ("z", "y"), ("x", "c")
    placed = (
        P(seq, mp),
        P(),
        P(None, None, seq, mp),
        P(None, None, None, mp),
        P(mp, None),
        P(mp, None),
        P(seq, mp),
    )
    return jax.shard_map(
        local,
        mesh=wide,
        in_specs=placed,
        out_specs=(P(seq, mp), P(seq, mp)),
        check_vma=False,
    )
```

```python
import functools

import jax
import jax.numpy as jnp
from jax import lax
from jax.experimental import pallas as pl
from jax.experimental.pallas import tpu as pltpu
from jax.sharding import Mesh, PartitionSpec as P

AXES = ("z", "y", "x", "c")
MIB = 2**20
SHORT_CALL = pl.CostEstimate(flops=1, bytes_accessed=1, transcendentals=0)
SMALL = pltpu.CompilerParams(vmem_limit_bytes=10 * MIB)


def factors(mesh):
    seq, mp = mesh.shape["seq"], mesh.shape["mp"]
    along_y = 1
    while 2 * along_y * along_y < seq:
        along_y *= 2
    return seq // along_y, along_y, mp // 2, 2


def rotate(value, axis, by):
    size = lax.axis_size(axis)
    return lax.ppermute(value, axis, [(i, (i + by) % size) for i in range(size)])


class Steps:
    def __init__(self):
        self.gate, self.open = (), []

    def __call__(self, send, value, *earlier, wait=True):
        found = send(after(value, *self.gate, *earlier))
        if wait:
            self.open.append(found)
        return found

    def then(self, *others):
        self.gate, self.open = tuple(self.open) + others, []


def after(value, *earlier):
    return lax.optimization_barrier((value, *earlier))[0]


def split_kernel(source, gain, target):
    target[0] = (source[0, 0].astype(jnp.float32) * gain[...]).astype(jnp.bfloat16)


def split_weights(in_weight, block, c, gain):
    parts = lax.axis_size("z")
    rows, columns = in_weight.shape[2], in_weight.shape[3] // parts
    if columns % 128:
        scaled = (in_weight[block, c].astype(jnp.float32) * gain).astype(jnp.bfloat16)
        return scaled.reshape(rows, parts, columns).transpose(1, 0, 2)
    return pl.pallas_call(
        split_kernel,
        grid=(parts,),
        in_specs=[
            pl.BlockSpec((1, 1, rows, columns), lambda k: (block, c, 0, k)),
            pl.BlockSpec((rows, 1), lambda k: (0, 0)),
        ],
        out_specs=pl.BlockSpec((1, rows, columns), lambda k: (k, 0, 0)),
        cost_estimate=SHORT_CALL,
        compiler_params=pltpu.CompilerParams(vmem_limit_bytes=10 * MIB),
        out_shape=jax.ShapeDtypeStruct((parts, rows, columns), jnp.bfloat16),
    )(in_weight, gain)


def exchange(pieces):
    return lax.all_to_all(pieces, "z", 0, 0, tiled=True)


def others(axis, value, send):
    moves = [functools.partial(rotate, axis=axis, by=j) for j in range(1, lax.axis_size(axis))]
    return [value] + [send(move, value) for move in moves]


def at_once(move, value):
    return move(value)


def slot_of(z_from, x_at, c_at):
    x_size, c_size = lax.axis_size("x"), lax.axis_size("c")
    x_from, c_from = z_from // c_size, z_from % c_size
    return ((x_at - x_from) % x_size) * c_size + (c_at - c_from) % c_size


def joined_kernel(blocks, place_ref, tokens_ref, *refs):
    firsts, rows = refs[:blocks], refs[blocks:-5]
    out_ref, first_held, rows_held, first_came, rows_came = refs[-5:]
    parts = place_ref.shape[0] // 2
    y_size = len(rows) // parts
    deep = rows[0].shape[0]

    def first_arrival(r):
        return pltpu.make_async_copy(firsts[r], first_held.at[r], first_came.at[r])

    def rows_arrival(n):
        return pltpu.make_async_copy(rows[n], rows_held.at[n], rows_came.at[n])

    for r in range(blocks):
        first_arrival(r).start()
    for n in range(len(rows)):
        rows_arrival(n).start()
    for r in range(blocks):
        first_arrival(r).wait()
    total = tokens_ref[...].astype(jnp.float32)
    for n in range(len(rows)):
        rows_arrival(n).wait()
        begin = pl.multiple_of(place_ref[parts + n % y_size] * deep, deep)
        total = total + jnp.dot(
            first_held[place_ref[n // y_size], :, pl.ds(begin, deep)], rows_held[n], preferred_element_type=jnp.float32
        )
    out_ref[...] = total.astype(out_ref.dtype)


def joined(tokens, first, held, places, where):
    _, y_at, x_at, c_at = where
    parts, y_size = len(held), len(held[0])
    place = [slot_of(p, x_at, c_at) for p in places] + [(y_at - j) % y_size for j in range(y_size)]
    place += [y_at * 0] * (2 * parts - len(place))
    rows = [w for group in held for w in group]
    anywhere = pl.BlockSpec(memory_space=pl.ANY)
    return pl.pallas_call(
        functools.partial(joined_kernel, len(first)),
        grid_spec=pltpu.PrefetchScalarGridSpec(
            num_scalar_prefetch=1,
            grid=(1,),
            in_specs=[pl.BlockSpec(tokens.shape, lambda i, place: (0, 0))] + [anywhere] * (len(first) + len(rows)),
            out_specs=pl.BlockSpec(tokens.shape, lambda i, place: (0, 0)),
            scratch_shapes=[
                pltpu.VMEM((len(first),) + first[0].shape, jnp.bfloat16),
                pltpu.VMEM((len(rows),) + rows[0].shape, jnp.bfloat16),
                pltpu.SemaphoreType.DMA((len(first),)),
                pltpu.SemaphoreType.DMA((len(rows),)),
            ],
        ),
        out_shape=jax.ShapeDtypeStruct(tokens.shape, tokens.dtype),
        compiler_params=pltpu.CompilerParams(vmem_limit_bytes=60 * MIB),
    )(jnp.stack(place).astype(jnp.int32), tokens, *first, *rows)


def all_of_c(found):
    return [rotate(p, "c", d) if d else p for p in found for d in range(lax.axis_size("c"))]


def next_along_z(value):
    return rotate(value, "z", 1)


def project_kernel(groups, order_ref, *refs):
    count = len(refs) - 5
    pieces = refs[: count - 3 * (order_ref.shape[0] - groups[1])]
    weights = refs[len(pieces) : count]
    out_ref, held, total, squares, arrived = refs[-5:]
    step = pl.program_id(0)
    y_size = len(weights) // 3
    deep, width = weights[0].shape[1], weights[0].shape[2]
    rows = pieces[0].shape[0]

    def arrival(g, r):
        return pltpu.make_async_copy(
            pieces[g * groups[1] + r], held.at[r, pl.ds(g * rows, rows)], arrived.at[r, g]
        )

    @pl.when(step == 0)
    def _():
        for r in range(groups[1]):
            for g in range(groups[0]):
                arrival(g, r).start()
        total[...] = jnp.zeros_like(total)
        squares[...] = jnp.zeros_like(squares)

    for r in range(groups[1]):

        @pl.when(step == r)
        def _(r=r):
            for g in range(groups[0]):
                arrival(g, r).wait()

    for g in range(groups[0]):
        these = slice(g * rows, (g + 1) * rows)
        values = held[step, these].astype(jnp.float32)
        squares[these] += jnp.sum(values * values, axis=1, keepdims=True)
    for c in range(3):
        some = 0.0
        for j in range(y_size):
            begin = pl.multiple_of(order_ref[groups[1] + j] * deep, deep)
            some = some + jnp.dot(
                held[step, :, pl.ds(begin, deep)], weights[c * y_size + j][0], preferred_element_type=jnp.float32
            )
        total[:, c * width : (c + 1) * width] += some

    @pl.when(step == groups[1] - 1)
    def _():
        scale = lax.rsqrt(squares[...] / (groups[1] * pieces[0].shape[1]) + 1e-06)
        out_ref[...] = (total[...] * scale).astype(out_ref.dtype)


def project(found, weights, order):
    groups = (len(found), len(found[0]))
    flat = [w for group in weights for w in group]
    pieces = [p for group in found for p in group]
    rows, features_here = pieces[0].shape
    width = flat[0].shape[2]
    needed = groups[0] * rows * (groups[1] * features_here * 2 + 3 * width * 8 + 512) + 12 * flat[0][0].size * len(flat) // 3
    out = pl.pallas_call(
        functools.partial(project_kernel, groups),
        grid_spec=pltpu.PrefetchScalarGridSpec(
            num_scalar_prefetch=1,
            grid=(groups[1],),
            in_specs=[pl.BlockSpec(memory_space=pl.ANY)] * len(pieces)
            + [pl.BlockSpec((1,) + w.shape[1:], lambda r, order: (order[r], 0, 0)) for w in flat],
            out_specs=pl.BlockSpec((groups[0] * rows, 3 * width), lambda r, order: (0, 0)),
            scratch_shapes=[
                pltpu.VMEM((groups[1], groups[0] * rows, features_here), jnp.bfloat16),
                pltpu.VMEM((groups[0] * rows, 3 * width), jnp.float32),
                pltpu.VMEM((groups[0] * rows, 1), jnp.float32),
                pltpu.SemaphoreType.DMA((groups[1], groups[0])),
            ],
        ),
        out_shape=jax.ShapeDtypeStruct((groups[0] * rows, 3 * width), jnp.bfloat16),
        compiler_params=pltpu.CompilerParams(vmem_limit_bytes=60 * MIB),
    )(order, *pieces, *flat)
    return out.reshape(groups[0], rows, 3 * width)


def mix_table(z_at, y_at, places):
    parts = len(places)
    stacked = jnp.stack(places)
    behind = jnp.where(y_at == 0, stacked[(stacked - 1) % parts], jnp.arange(parts))
    some = jnp.where((y_at == 0) & (stacked == 0), 0, 1)
    return jnp.stack([behind, some, stacked]).astype(jnp.int32)


def delayed(value, by):
    return pltpu.roll(value, by, 0) if by else value


def taps_sum(value, taps):
    total = taps[0] * value
    for s in range(1, len(taps)):
        total = total + taps[s] * delayed(value, s)
    return total


def features(lanes, width, start, table_ref, proj_ref, before_ref, feat_ref):
    some = table_ref[1, pl.program_id(0)].astype(jnp.float32)
    out = []
    for c in range(3):
        begin = c * width + start
        before = before_ref[0, :, begin : begin + lanes].astype(jnp.float32) * some
        value = jnp.concatenate([before, proj_ref[0, :, begin : begin + lanes].astype(jnp.float32)], axis=0)
        taps = [feat_ref[c, s : s + 1, start : start + lanes] for s in range(feat_ref.shape[1])]
        out.append(taps_sum(value, taps))
    return out


def short_kernel(table_ref, proj_ref, before_ref, feat_ref, taps_ref, out_ref):
    width = out_ref.shape[2]
    lanes = min(128, width)
    rim = before_ref.shape[1]
    for start in range(0, width, lanes):
        query, key, value = features(lanes, width, start, table_ref, proj_ref, before_ref, feat_ref)
        kv = (key * value).astype(jnp.bfloat16).astype(jnp.float32)
        taps = [taps_ref[s : s + 1, start : start + lanes] for s in range(taps_ref.shape[0])]
        inner = taps_sum(kv, taps)
        out_ref[0, :, start : start + lanes] = (query[rim:] * inner[rim:]).astype(out_ref.dtype)


def gate_kernel(table_ref, proj_ref, before_ref, feat_ref, query_ref, kv_ref):
    width = kv_ref.shape[2]
    lanes = min(128, width)
    rim = before_ref.shape[1]
    for start in range(0, width, lanes):
        query, key, value = features(lanes, width, start, table_ref, proj_ref, before_ref, feat_ref)
        query_ref[0, :, start : start + lanes] = query[rim:]
        kv_ref[0, :, start : start + lanes] = (key[rim:] * value[rim:]).astype(kv_ref.dtype)


def medium_kernel(table_ref, query_ref, kv_ref, before_ref, matrix_ref, out_ref):
    groups, span = matrix_ref.shape[0], matrix_ref.shape[1]
    count, width = out_ref.shape[1], out_ref.shape[2]
    lanes = min(128, width)
    per_group = width // groups
    some = table_ref[1, pl.program_id(0)]
    before = before_ref[0]
    before = jnp.where(some > 0, before, jnp.zeros_like(before))
    lane = lax.broadcasted_iota(jnp.int32, (span, lanes), 1) // per_group
    for block in range(count // span):
        own = kv_ref[0, block * span : (block + 1) * span]
        pair = jnp.concatenate([before, own], axis=0)
        before = own
        rows = slice(block * span, (block + 1) * span)
        for start in range(0, width, lanes):
            inner = jnp.zeros((span, lanes), jnp.float32)
            for g in range(lanes // per_group):
                taken = jnp.dot(
                    matrix_ref[start // per_group + g], pair[:, start : start + lanes], preferred_element_type=jnp.float32
                )
                inner = jnp.where(lane == g, taken, inner)
            query = query_ref[0, rows, start : start + lanes]
            out_ref[0, rows, start : start + lanes] = (query * inner).astype(out_ref.dtype)


def whole_spec(value):
    return pl.BlockSpec(value.shape, lambda i, table: (0,) * value.ndim)


def piece_spec(value, which=None):
    def index(i, table):
        return (i if which is None else table[which, i], 0, 0)

    return pl.BlockSpec((1,) + value.shape[1:], index)


def tails(pieces, count):
    return rotate(pieces[:, pieces.shape[1] - count :], "y", 1)


def short_mix(proj, before, feat, taps, table):
    out = jax.ShapeDtypeStruct(proj.shape[:2] + (proj.shape[2] // 3,), jnp.bfloat16)
    return pl.pallas_call(
        short_kernel,
        grid_spec=pltpu.PrefetchScalarGridSpec(
            num_scalar_prefetch=1,
            grid=(proj.shape[0],),
            in_specs=[piece_spec(proj), piece_spec(before, 0), whole_spec(feat), whole_spec(taps)],
            out_specs=piece_spec(out),
        ),
        cost_estimate=SHORT_CALL,
        compiler_params=SMALL,
        out_shape=out,
    )(table, proj, before, feat, taps)


def gate(proj, before, feat, table):
    shape = proj.shape[:2] + (proj.shape[2] // 3,)
    query = jax.ShapeDtypeStruct(shape, jnp.float32)
    kv = jax.ShapeDtypeStruct(shape, jnp.bfloat16)
    return pl.pallas_call(
        gate_kernel,
        grid_spec=pltpu.PrefetchScalarGridSpec(
            num_scalar_prefetch=1,
            grid=(proj.shape[0],),
            in_specs=[piece_spec(proj), piece_spec(before, 0), whole_spec(feat)],
            out_specs=[piece_spec(query), piece_spec(kv)],
        ),
        cost_estimate=SHORT_CALL,
        compiler_params=SMALL,
        out_shape=[query, kv],
    )(table, proj, before, feat)


def medium_mix(early, last, feat, matrix, table, z_at):
    parts, span = table.shape[1], matrix.shape[1]
    near_early, near_last = tails(early, 16), tails(last, 16)
    inside = jnp.minimum(table[:, : parts - 1], parts - 2)
    query, kv = gate(after(early, last), near_early, feat, inside)
    far_early = tails(kv, span)
    close = medium(query, kv, far_early, matrix, table[:, : parts - 2])
    made = [close[k] for k in range(parts - 2)]
    query, kv = gate(
        jnp.concatenate([early[-1:], last]), jnp.concatenate([near_early, near_last]), feat, table[:, parts - 2 :]
    )
    far = jnp.concatenate([far_early, tails(kv[1:], span)])
    distant = medium(query, kv, far, matrix, table[:, parts - 2 :])
    return home(made + [distant[0], distant[1]], z_at)


def medium(query, kv, before, matrix, table):
    count = table.shape[1]
    shape = (count,) + kv.shape[1:]
    return pl.pallas_call(
        medium_kernel,
        grid_spec=pltpu.PrefetchScalarGridSpec(
            num_scalar_prefetch=1,
            grid=(count,),
            in_specs=[piece_spec(query), piece_spec(kv), piece_spec(before, 0), whole_spec(matrix)],
            out_specs=piece_spec(kv),
        ),
        cost_estimate=SHORT_CALL,
        compiler_params=SMALL,
        out_shape=jax.ShapeDtypeStruct(shape, jnp.bfloat16),
    )(table, query, kv, before, matrix)


def toeplitz_kernel(row_ref, out_ref):
    width = out_ref.shape[1]
    rows = jnp.broadcast_to(row_ref[0], (width, 3 * width))
    turned = pltpu.roll(rows, 0, 1, stride=1, stride_axis=0)
    out_ref[0] = turned[:, : 2 * width].astype(out_ref.dtype)


def toeplitz(filt):
    groups, width = filt.shape
    row = jnp.concatenate([jnp.zeros((groups, 1)), filt[:, ::-1], jnp.zeros((groups, 2 * width - 1))], axis=1)[:, None]
    return pl.pallas_call(
        toeplitz_kernel,
        grid=(groups,),
        in_specs=[pl.BlockSpec((1, 1, 3 * width), lambda g: (g, 0, 0))],
        out_specs=pl.BlockSpec((1, width, 2 * width), lambda g: (g, 0, 0)),
        cost_estimate=SHORT_CALL,
        compiler_params=SMALL,
        out_shape=jax.ShapeDtypeStruct((groups, width, 2 * width), jnp.bfloat16),
    )(row)


def channels_of(value, z_at, axis):
    size = value.shape[axis] // lax.axis_size("z")
    return lax.dynamic_slice_in_dim(value, z_at * size, size, axis)


def home(pieces, z_at):
    parts = len(pieces)
    stacked = jnp.stack([rotate(piece, "z", -k) if k else piece for k, piece in enumerate(pieces)])
    ordered = [lax.dynamic_index_in_dim(stacked, (k - z_at) % parts, 0, keepdims=False) for k in range(parts)]
    return jnp.concatenate(ordered, axis=1)


def local(tokens, norm_gain, in_weight, feat_filter, short_filter, medium_filter, out_weight):
    where = tuple(lax.axis_index(a) for a in AXES)
    z_at, y_at, x_at, c_at = where
    parts = lax.axis_size("z")
    rows = in_weight.shape[2]
    width = in_weight.shape[3] // parts
    begin = (z_at * lax.axis_size("y") + y_at) * rows
    gains = lax.dynamic_slice_in_dim(norm_gain, begin, rows, 1)[:, :, None]
    feat = channels_of(feat_filter, z_at, 3)
    short = channels_of(short_filter, z_at, 0)
    short_taps = jnp.repeat(short.T, width // short.shape[0], axis=1)
    matrix = toeplitz(channels_of(medium_filter, z_at, 0))
    places = [(z_at - k) % parts for k in range(parts)]
    table = mix_table(z_at, y_at, places)
    x_size, c_size, y_size = (lax.axis_size(a) for a in ("x", "c", "y"))
    order = [((x_at - d) % x_size) * c_size + (c_at - e) % c_size for d in range(x_size) for e in range(c_size)]
    order = jnp.stack(order + [(y_at - j) % y_size for j in range(y_size)]).astype(jnp.int32)

    def split(block, c):
        return split_weights(in_weight, block, c, gains[block])

    step = Steps()
    ring, found, came, weights = [tokens], [], [], []
    rows_ring, held = [out_weight], []
    splits = [split(1, c) for c in range(3)]
    for k in range(parts):
        if k < parts - 1:
            ring.append(step(next_along_z, ring[k]))
        else:
            rows_ring.append(step(next_along_z, out_weight))
        if k < 3:
            came.append(step(exchange, split(0, k)))
        found.append([others("c", ring[k], step)])
        fresh = others("x", ring[k], step)[1:]
        if k:
            found[k - 1] += [others("c", piece, step) for piece in waiting]
        waiting = fresh
        if k == 0:
            held.append(others("y", out_weight, step))
        elif k <= 3:
            weights.append(others("y", came[k - 1], step))
        step.then(*([matrix] if k == 1 else splits if k == 2 else []))
    found[-1] += [others("c", piece, at_once) for piece in waiting]
    proj = project([sum(group, []) for group in found], weights, order)
    near = tails(after(proj, *step.gate), 16)
    for k in range(1, parts - 1):
        rows_ring.append(step(next_along_z, rows_ring[k]))
        held.append(others("y", after(rows_ring[k], near) if k == parts - 2 else rows_ring[k], step))
        step.then(proj)
    gated = short_mix(proj, near, feat[0], short_taps, table)
    gated = after(gated, rows_ring[-1], *held[-1])
    back = home([gated[k] for k in range(parts)], z_at)
    held.append(others("y", after(rows_ring[-1], *held[-1]), at_once))
    first = all_of_c([after(piece, *held[-1]) for piece in others("x", back, at_once)])
    step.then(*step.gate, back)
    came, weights_next = [step(exchange, splits[0])], []
    came.append(exchange(after(splits[1], came[0], *first)))
    stream = joined(tokens, first, held, places, where)

    step.then(stream)
    ring, found, swapped = [stream], [], []

    def swap(k):
        found.append([others("c", ring[k], step)])
        swapped.append(others("x", ring[k], step)[1:])

    def spread(k):
        found[k] += [others("c", piece, step) for piece in swapped[k]]

    ring.append(step(next_along_z, ring[0]))
    weights_next.append(others("y", came[0], step))
    swap(0)
    step.then()
    came.append(step(exchange, splits[2]))
    weights_next.append(others("y", came[1], step))
    swap(1)
    spread(0)
    step.then()
    for k in range(2, parts):
        ring.append(step(next_along_z, ring[k - 1]))
        if k == 2:
            weights_next.append(others("y", came[2], functools.partial(step, wait=False)))
        else:
            swap(k - 1)
        spread(k - 1 if k == 2 else k - 2) if k != 3 else None
        step.then()
    early = project([sum(group, []) for group in found[:2]], weights_next, order)
    step.then(*step.gate, early)
    spread(parts - 2)
    count = stream.shape[0]
    half = count // 2
    near_half = others("x", ring[-1][:half], step)[1:]
    far_half = [step(next_along_z, piece[half:]) for piece in swapped[-1]]
    halves = [[others("c", ring[-1][:half], at_once)], [others("c", ring[-1][half:], at_once)]]
    early = [early] + [project([sum(group, [])], weights_next, order) for group in found[2:]]
    early = jnp.concatenate(early)
    for group, more in zip(halves, (near_half, far_half)):
        group += [others("c", after(piece, early), at_once) for piece in more]
    last = project([sum(group, []) for group in halves], weights_next, order).reshape(1, count, -1)
    return stream, medium_mix(early, last, feat[1], matrix, table, z_at)


def solution(mesh):
    wide = Mesh(mesh.devices.reshape(factors(mesh)), AXES)
    seq, mp = ("z", "y"), ("x", "c")
    placed = (
        P(seq, mp),
        P(),
        P(None, None, seq, mp),
        P(None, None, None, mp),
        P(mp, None),
        P(mp, None),
        P(seq, mp),
    )
    return jax.shard_map(
        local,
        mesh=wide,
        in_specs=placed,
        out_specs=(P(seq, mp), P(seq, mp)),
        check_vma=False,
    )
```

```python
import functools

import jax
import jax.numpy as jnp
from jax import lax
from jax.experimental import pallas as pl
from jax.experimental.pallas import tpu as pltpu
from jax.sharding import Mesh, PartitionSpec as P

AXES = ("z", "y", "x", "c")
MIB = 2**20
SHORT_CALL = pl.CostEstimate(flops=1, bytes_accessed=1, transcendentals=0)
SMALL = pltpu.CompilerParams(vmem_limit_bytes=10 * MIB)


def factors(mesh):
    seq, mp = mesh.shape["seq"], mesh.shape["mp"]
    along_y = 1
    while 2 * along_y * along_y < seq:
        along_y *= 2
    return seq // along_y, along_y, mp // 2, 2


def rotate(value, axis, by):
    size = lax.axis_size(axis)
    return lax.ppermute(value, axis, [(i, (i + by) % size) for i in range(size)])


class Steps:
    def __init__(self):
        self.gate, self.open = (), []

    def __call__(self, send, value, *earlier, wait=True):
        found = send(after(value, *self.gate, *earlier))
        if wait:
            self.open.append(found)
        return found

    def then(self, *others):
        self.gate, self.open = tuple(self.open) + others, []


def after(value, *earlier):
    return lax.optimization_barrier((value, *earlier))[0]


def split_kernel(source, gain, target):
    target[0] = (source[0, 0].astype(jnp.float32) * gain[...]).astype(jnp.bfloat16)


def split_weights(in_weight, block, c, gain):
    parts = lax.axis_size("z")
    rows, columns = in_weight.shape[2], in_weight.shape[3] // parts
    if columns % 128:
        scaled = (in_weight[block, c].astype(jnp.float32) * gain).astype(jnp.bfloat16)
        return scaled.reshape(rows, parts, columns).transpose(1, 0, 2)
    return pl.pallas_call(
        split_kernel,
        grid=(parts,),
        in_specs=[
            pl.BlockSpec((1, 1, rows, columns), lambda k: (block, c, 0, k)),
            pl.BlockSpec((rows, 1), lambda k: (0, 0)),
        ],
        out_specs=pl.BlockSpec((1, rows, columns), lambda k: (k, 0, 0)),
        cost_estimate=SHORT_CALL,
        compiler_params=pltpu.CompilerParams(vmem_limit_bytes=10 * MIB),
        out_shape=jax.ShapeDtypeStruct((parts, rows, columns), jnp.bfloat16),
    )(in_weight, gain)


def exchange(pieces):
    return lax.all_to_all(pieces, "z", 0, 0, tiled=True)


def others(axis, value, send):
    moves = [functools.partial(rotate, axis=axis, by=j) for j in range(1, lax.axis_size(axis))]
    return [value] + [send(move, value) for move in moves]


def at_once(move, value):
    return move(value)


def slot_of(z_from, x_at, c_at):
    x_size, c_size = lax.axis_size("x"), lax.axis_size("c")
    x_from, c_from = z_from // c_size, z_from % c_size
    return ((x_at - x_from) % x_size) * c_size + (c_at - c_from) % c_size


def joined_kernel(blocks, place_ref, tokens_ref, *refs):
    firsts, rows = refs[:blocks], refs[blocks:-5]
    out_ref, first_held, rows_held, first_came, rows_came = refs[-5:]
    parts = place_ref.shape[0] // 2
    y_size = len(rows) // parts
    deep = rows[0].shape[0]

    def first_arrival(r):
        return pltpu.make_async_copy(firsts[r], first_held.at[r], first_came.at[r])

    def rows_arrival(n):
        return pltpu.make_async_copy(rows[n], rows_held.at[n], rows_came.at[n])

    for r in range(blocks):
        first_arrival(r).start()
    for n in range(len(rows)):
        rows_arrival(n).start()
    for r in range(blocks):
        first_arrival(r).wait()
    total = tokens_ref[...].astype(jnp.float32)
    for n in range(len(rows)):
        rows_arrival(n).wait()
        begin = pl.multiple_of(place_ref[parts + n % y_size] * deep, deep)
        total = total + jnp.dot(
            first_held[place_ref[n // y_size], :, pl.ds(begin, deep)], rows_held[n], preferred_element_type=jnp.float32
        )
    out_ref[...] = total.astype(out_ref.dtype)


def joined(tokens, first, held, places, where):
    _, y_at, x_at, c_at = where
    parts, y_size = len(held), len(held[0])
    place = [slot_of(p, x_at, c_at) for p in places] + [(y_at - j) % y_size for j in range(y_size)]
    place += [y_at * 0] * (2 * parts - len(place))
    rows = [w for group in held for w in group]
    anywhere = pl.BlockSpec(memory_space=pl.ANY)
    return pl.pallas_call(
        functools.partial(joined_kernel, len(first)),
        grid_spec=pltpu.PrefetchScalarGridSpec(
            num_scalar_prefetch=1,
            grid=(1,),
            in_specs=[pl.BlockSpec(tokens.shape, lambda i, place: (0, 0))] + [anywhere] * (len(first) + len(rows)),
            out_specs=pl.BlockSpec(tokens.shape, lambda i, place: (0, 0)),
            scratch_shapes=[
                pltpu.VMEM((len(first),) + first[0].shape, jnp.bfloat16),
                pltpu.VMEM((len(rows),) + rows[0].shape, jnp.bfloat16),
                pltpu.SemaphoreType.DMA((len(first),)),
                pltpu.SemaphoreType.DMA((len(rows),)),
            ],
        ),
        out_shape=jax.ShapeDtypeStruct(tokens.shape, tokens.dtype),
        compiler_params=pltpu.CompilerParams(vmem_limit_bytes=60 * MIB),
    )(jnp.stack(place).astype(jnp.int32), tokens, *first, *rows)


def all_of_c(found):
    return [rotate(p, "c", d) if d else p for p in found for d in range(lax.axis_size("c"))]


def next_along_z(value):
    return rotate(value, "z", 1)


def project_kernel(groups, kept, order_ref, *refs):
    count = len(refs) - 5
    pieces = refs[: count - 3 * (order_ref.shape[0] - groups[1])]
    weights = refs[len(pieces) : count]
    out_ref, held, total, squares, arrived = refs[-5:]
    step = pl.program_id(0)
    y_size = len(weights) // 3
    deep, width = weights[0].shape[1], weights[0].shape[2]
    rows = pieces[0].shape[0]

    def arrival(g, r):
        return pltpu.make_async_copy(
            pieces[g * groups[1] + r], held.at[r, pl.ds(g * rows, rows)], arrived.at[r, g]
        )

    @pl.when(step == 0)
    def _():
        for r in range(groups[1]):
            for g in range(groups[0]):
                arrival(g, r).start()
        total[...] = jnp.zeros_like(total)
        squares[...] = jnp.zeros_like(squares)

    for r in range(groups[1]):

        @pl.when(step == r)
        def _(r=r):
            for g in range(groups[0]):
                arrival(g, r).wait()

    for g in range(groups[0]):
        these = slice(g * rows, (g + 1) * rows)
        values = held[step, these].astype(jnp.float32)
        squares[these] += jnp.sum(values * values, axis=1, keepdims=True)
    for c in range(3):
        some = 0.0
        for j in range(y_size):
            begin = pl.multiple_of(order_ref[groups[1] + j] * deep, deep)
            some = some + jnp.dot(
                held[step, :, pl.ds(begin, deep)], weights[c * y_size + j][order_ref[step] if kept else 0], preferred_element_type=jnp.float32
            )
        total[:, c * width : (c + 1) * width] += some

    @pl.when(step == groups[1] - 1)
    def _():
        scale = lax.rsqrt(squares[...] / (groups[1] * pieces[0].shape[1]) + 1e-06)
        out_ref[...] = (total[...] * scale).astype(out_ref.dtype)


def project(found, weights, order, kept=False):
    groups = (len(found), len(found[0]))
    flat = [w for group in weights for w in group]
    pieces = [p for group in found for p in group]
    rows, features_here = pieces[0].shape
    width = flat[0].shape[2]
    needed = groups[0] * rows * (groups[1] * features_here * 2 + 3 * width * 8 + 512) + 12 * flat[0][0].size * len(flat) // 3
    out = pl.pallas_call(
        functools.partial(project_kernel, groups, kept),
        grid_spec=pltpu.PrefetchScalarGridSpec(
            num_scalar_prefetch=1,
            grid=(groups[1],),
            in_specs=[pl.BlockSpec(memory_space=pl.ANY)] * len(pieces)
            + [
                pl.BlockSpec(memory_space=pltpu.VMEM)
                if kept
                else pl.BlockSpec((1,) + w.shape[1:], lambda r, order: (order[r], 0, 0))
                for w in flat
            ],
            out_specs=pl.BlockSpec((groups[0] * rows, 3 * width), lambda r, order: (0, 0)),
            scratch_shapes=[
                pltpu.VMEM((groups[1], groups[0] * rows, features_here), jnp.bfloat16),
                pltpu.VMEM((groups[0] * rows, 3 * width), jnp.float32),
                pltpu.VMEM((groups[0] * rows, 1), jnp.float32),
                pltpu.SemaphoreType.DMA((groups[1], groups[0])),
            ],
        ),
        out_shape=jax.ShapeDtypeStruct((groups[0] * rows, 3 * width), jnp.bfloat16),
        compiler_params=pltpu.CompilerParams(vmem_limit_bytes=(30 * MIB) if kept else 60 * MIB),
    )(order, *pieces, *flat)
    return out.reshape(groups[0], rows, 3 * width)


def mix_table(z_at, y_at, places):
    parts = len(places)
    stacked = jnp.stack(places)
    behind = jnp.where(y_at == 0, stacked[(stacked - 1) % parts], jnp.arange(parts))
    some = jnp.where((y_at == 0) & (stacked == 0), 0, 1)
    return jnp.stack([behind, some, stacked]).astype(jnp.int32)


def delayed(value, by):
    return pltpu.roll(value, by, 0) if by else value


def taps_sum(value, taps):
    total = taps[0] * value
    for s in range(1, len(taps)):
        total = total + taps[s] * delayed(value, s)
    return total


def features(lanes, width, start, table_ref, proj_ref, before_ref, feat_ref):
    some = table_ref[1, pl.program_id(0)].astype(jnp.float32)
    out = []
    for c in range(3):
        begin = c * width + start
        before = before_ref[0, :, begin : begin + lanes].astype(jnp.float32) * some
        value = jnp.concatenate([before, proj_ref[0, :, begin : begin + lanes].astype(jnp.float32)], axis=0)
        taps = [feat_ref[c, s : s + 1, start : start + lanes] for s in range(feat_ref.shape[1])]
        out.append(taps_sum(value, taps))
    return out


def short_kernel(table_ref, proj_ref, before_ref, feat_ref, taps_ref, out_ref):
    width = out_ref.shape[2]
    lanes = min(128, width)
    rim = before_ref.shape[1]
    for start in range(0, width, lanes):
        query, key, value = features(lanes, width, start, table_ref, proj_ref, before_ref, feat_ref)
        kv = (key * value).astype(jnp.bfloat16).astype(jnp.float32)
        taps = [taps_ref[s : s + 1, start : start + lanes] for s in range(taps_ref.shape[0])]
        inner = taps_sum(kv, taps)
        out_ref[0, :, start : start + lanes] = (query[rim:] * inner[rim:]).astype(out_ref.dtype)


def gate_kernel(table_ref, proj_ref, before_ref, feat_ref, query_ref, kv_ref):
    width = kv_ref.shape[2]
    lanes = min(128, width)
    rim = before_ref.shape[1]
    for start in range(0, width, lanes):
        query, key, value = features(lanes, width, start, table_ref, proj_ref, before_ref, feat_ref)
        query_ref[0, :, start : start + lanes] = query[rim:]
        kv_ref[0, :, start : start + lanes] = (key[rim:] * value[rim:]).astype(kv_ref.dtype)


def medium_kernel(table_ref, query_ref, kv_ref, before_ref, matrix_ref, out_ref):
    groups, span = matrix_ref.shape[0], matrix_ref.shape[1]
    count, width = out_ref.shape[1], out_ref.shape[2]
    lanes = min(128, width)
    per_group = width // groups
    some = table_ref[1, pl.program_id(0)]
    before = before_ref[0]
    before = jnp.where(some > 0, before, jnp.zeros_like(before))
    lane = lax.broadcasted_iota(jnp.int32, (span, lanes), 1) // per_group
    for block in range(count // span):
        own = kv_ref[0, block * span : (block + 1) * span]
        pair = jnp.concatenate([before, own], axis=0)
        before = own
        rows = slice(block * span, (block + 1) * span)
        for start in range(0, width, lanes):
            inner = jnp.zeros((span, lanes), jnp.float32)
            for g in range(lanes // per_group):
                taken = jnp.dot(
                    matrix_ref[start // per_group + g], pair[:, start : start + lanes], preferred_element_type=jnp.float32
                )
                inner = jnp.where(lane == g, taken, inner)
            query = query_ref[0, rows, start : start + lanes]
            out_ref[0, rows, start : start + lanes] = (query * inner).astype(out_ref.dtype)


def whole_spec(value):
    return pl.BlockSpec(value.shape, lambda i, table: (0,) * value.ndim)


def piece_spec(value, which=None):
    def index(i, table):
        return (i if which is None else table[which, i], 0, 0)

    return pl.BlockSpec((1,) + value.shape[1:], index)


def tails(pieces, count):
    return rotate(pieces[:, pieces.shape[1] - count :], "y", 1)


def short_mix(proj, before, feat, taps, table):
    out = jax.ShapeDtypeStruct(proj.shape[:2] + (proj.shape[2] // 3,), jnp.bfloat16)
    return pl.pallas_call(
        short_kernel,
        grid_spec=pltpu.PrefetchScalarGridSpec(
            num_scalar_prefetch=1,
            grid=(proj.shape[0],),
            in_specs=[piece_spec(proj), piece_spec(before, 0), whole_spec(feat), whole_spec(taps)],
            out_specs=piece_spec(out),
        ),
        cost_estimate=SHORT_CALL,
        compiler_params=SMALL,
        out_shape=out,
    )(table, proj, before, feat, taps)


def gate(proj, before, feat, table):
    shape = proj.shape[:2] + (proj.shape[2] // 3,)
    query = jax.ShapeDtypeStruct(shape, jnp.float32)
    kv = jax.ShapeDtypeStruct(shape, jnp.bfloat16)
    return pl.pallas_call(
        gate_kernel,
        grid_spec=pltpu.PrefetchScalarGridSpec(
            num_scalar_prefetch=1,
            grid=(proj.shape[0],),
            in_specs=[piece_spec(proj), piece_spec(before, 0), whole_spec(feat)],
            out_specs=[piece_spec(query), piece_spec(kv)],
        ),
        cost_estimate=SHORT_CALL,
        compiler_params=SMALL,
        out_shape=[query, kv],
    )(table, proj, before, feat)


def medium_early(early, feat, table, span):
    near = tails(early, 16)
    query, kv = gate(early, near, feat, jnp.minimum(table[:, :-1], table.shape[1] - 2))
    return near, query, kv, tails(kv, span)


def medium_mix(early, made_early, last, feat, matrix, table, z_at):
    parts, span = table.shape[1], matrix.shape[1]
    near_early, query, kv, far_early = made_early
    near = jnp.concatenate([near_early, tails(last, 16)])
    close = medium(after(query, last), kv, far_early, matrix, table[:, : parts - 2])
    both = after(jnp.concatenate([early[-1:], last]), close)
    query, kv = gate(both, near, feat, table[:, parts - 2 :])
    far = jnp.concatenate([far_early, tails(kv[1:], span)])
    distant = medium(query, kv, far, matrix, table[:, parts - 2 :])
    return home([close[k] for k in range(parts - 2)] + [distant[0], distant[1]], z_at)


def medium(query, kv, before, matrix, table):
    count = table.shape[1]
    shape = (count,) + kv.shape[1:]
    return pl.pallas_call(
        medium_kernel,
        grid_spec=pltpu.PrefetchScalarGridSpec(
            num_scalar_prefetch=1,
            grid=(count,),
            in_specs=[piece_spec(query), piece_spec(kv), piece_spec(before, 0), whole_spec(matrix)],
            out_specs=piece_spec(kv),
        ),
        cost_estimate=SHORT_CALL,
        compiler_params=SMALL,
        out_shape=jax.ShapeDtypeStruct(shape, jnp.bfloat16),
    )(table, query, kv, before, matrix)


def toeplitz_kernel(row_ref, out_ref):
    width = out_ref.shape[1]
    rows = jnp.broadcast_to(row_ref[0], (width, 3 * width))
    turned = pltpu.roll(rows, 0, 1, stride=1, stride_axis=0)
    out_ref[0] = turned[:, : 2 * width].astype(out_ref.dtype)


def toeplitz(filt):
    groups, width = filt.shape
    row = jnp.concatenate([jnp.zeros((groups, 1)), filt[:, ::-1], jnp.zeros((groups, 2 * width - 1))], axis=1)[:, None]
    return pl.pallas_call(
        toeplitz_kernel,
        grid=(groups,),
        in_specs=[pl.BlockSpec((1, 1, 3 * width), lambda g: (g, 0, 0))],
        out_specs=pl.BlockSpec((1, width, 2 * width), lambda g: (g, 0, 0)),
        cost_estimate=SHORT_CALL,
        compiler_params=SMALL,
        out_shape=jax.ShapeDtypeStruct((groups, width, 2 * width), jnp.bfloat16),
    )(row)


def channels_of(value, z_at, axis):
    size = value.shape[axis] // lax.axis_size("z")
    return lax.dynamic_slice_in_dim(value, z_at * size, size, axis)


def home(pieces, z_at):
    parts = len(pieces)
    stacked = jnp.stack([rotate(piece, "z", -k) if k else piece for k, piece in enumerate(pieces)])
    ordered = [lax.dynamic_index_in_dim(stacked, (k - z_at) % parts, 0, keepdims=False) for k in range(parts)]
    return jnp.concatenate(ordered, axis=1)


def local(tokens, norm_gain, in_weight, feat_filter, short_filter, medium_filter, out_weight):
    where = tuple(lax.axis_index(a) for a in AXES)
    z_at, y_at, x_at, c_at = where
    parts = lax.axis_size("z")
    rows = in_weight.shape[2]
    width = in_weight.shape[3] // parts
    begin = (z_at * lax.axis_size("y") + y_at) * rows
    gains = lax.dynamic_slice_in_dim(norm_gain, begin, rows, 1)[:, :, None]
    feat = channels_of(feat_filter, z_at, 3)
    short = channels_of(short_filter, z_at, 0)
    short_taps = jnp.repeat(short.T, width // short.shape[0], axis=1)
    matrix = toeplitz(channels_of(medium_filter, z_at, 0))
    places = [(z_at - k) % parts for k in range(parts)]
    table = mix_table(z_at, y_at, places)
    x_size, c_size, y_size = (lax.axis_size(a) for a in ("x", "c", "y"))
    order = [((x_at - d) % x_size) * c_size + (c_at - e) % c_size for d in range(x_size) for e in range(c_size)]
    order = jnp.stack(order + [(y_at - j) % y_size for j in range(y_size)]).astype(jnp.int32)

    def split(block, c):
        return split_weights(in_weight, block, c, gains[block])

    step = Steps()
    ring, found, came, weights = [tokens], [], [], []
    rows_ring, held = [out_weight], []
    splits = [[split(block, c) for c in range(3)] for block in range(2)]
    for k in range(parts):
        if k < parts - 1:
            ring.append(next_along_z(ring[k]))
        found.append([others("c", ring[k], step)])
        fresh = others("x", ring[k], step)[1:]
        own = found[k][0][1:]
        if k < 3:
            came.append(exchange(after(splits[0][k], *own, *came[-1:])))
        if k:
            found[k - 1] += [others("c", piece, step) for piece in waiting]
        waiting = fresh
        if k == 0:
            held.append(others("y", out_weight, step))
        elif k <= 3:
            weights.append(others("y", after(came[k - 1], *own), step))
        if k == parts - 1:
            rows_ring.append(step(next_along_z, after(out_weight, came[2])))
        step.then(*([splits[0][1:], splits[1] + [matrix], []] + [[]] * parts)[k])
    found[-1] += [others("c", piece, at_once) for piece in waiting]
    proj = project([sum(group, []) for group in found], weights, order)
    near = tails(after(proj, *step.gate), 16)
    for k in range(1, parts - 1):
        rows_ring.append(step(next_along_z, rows_ring[k]))
        held.append(others("y", after(rows_ring[k], near) if k == parts - 2 else rows_ring[k], step))
        step.then(proj)
    gated = short_mix(proj, near, feat[0], short_taps, table)
    gated = after(gated, rows_ring[-1], *held[-1])
    back = home([gated[k] for k in range(parts)], z_at)
    held.append(others("y", after(rows_ring[-1], *held[-1]), at_once))
    first = all_of_c([after(piece, *held[-1]) for piece in others("x", back, at_once)])
    step.then(*step.gate, back)
    came, weights_next = [step(exchange, splits[1][0])], []
    came.append(exchange(after(splits[1][1], came[0], *first)))
    stream = joined(tokens, first, held, places, where)

    step.then(stream)
    ring, found, swapped = [stream], [], []

    def swap(k):
        found.append([others("c", ring[k], step)])
        swapped.append(others("x", ring[k], step)[1:])

    def spread(k):
        found[k] += [others("c", piece, step) for piece in swapped[k]]

    ring.append(step(next_along_z, ring[0]))
    weights_next.append(others("y", came[0], step))
    swap(0)
    step.then()
    came.append(step(exchange, splits[1][2]))
    weights_next.append(others("y", came[1], step))
    swap(1)
    spread(0)
    step.then()
    for k in range(2, parts):
        ring.append(step(next_along_z, ring[k - 1]))
        if k == 2:
            weights_next.append(others("y", came[2], functools.partial(step, wait=False)))
        else:
            swap(k - 1)
        spread(k - 1 if k == 2 else k - 2) if k != 3 else None
        step.then()
    early = project([sum(group, []) for group in found[:2]], weights_next, order)
    step.then(*step.gate, early)
    spread(parts - 2)
    count = stream.shape[0]
    half = count // 2
    near_half = others("x", ring[-1][:half], step)[1:]
    far_half = [step(next_along_z, piece[half:]) for piece in swapped[-1]]
    halves = [[others("c", ring[-1][:half], at_once)], [others("c", ring[-1][half:], at_once)]]
    early = [early] + [project([sum(group, [])], weights_next, order, True) for group in found[2:]]
    early = jnp.concatenate(early)
    for group, more in zip(halves, (near_half, far_half)):
        group += [others("c", after(piece, early), at_once) for piece in more]
    made_early = medium_early(early, feat[1], table, matrix.shape[1])
    halves[0][0][0] = after(halves[0][0][0], made_early[2])
    last = project([sum(group, []) for group in halves], weights_next, order, True).reshape(1, count, -1)
    return stream, medium_mix(early, made_early, last, feat[1], matrix, table, z_at)


def solution(mesh):
    wide = Mesh(mesh.devices.reshape(factors(mesh)), AXES)
    seq, mp = ("z", "y"), ("x", "c")
    placed = (
        P(seq, mp),
        P(),
        P(None, None, seq, mp),
        P(None, None, None, mp),
        P(mp, None),
        P(mp, None),
        P(seq, mp),
    )
    return jax.shard_map(
        local,
        mesh=wide,
        in_specs=placed,
        out_specs=(P(seq, mp), P(seq, mp)),
        check_vma=False,
    )
```

```python
import functools

import jax
import jax.numpy as jnp
from jax import lax
from jax.experimental import pallas as pl
from jax.experimental.pallas import tpu as pltpu
from jax.sharding import Mesh, PartitionSpec as P

AXES = ("z", "y", "x", "c")
MIB = 2**20
SHORT_CALL = pl.CostEstimate(flops=1, bytes_accessed=1, transcendentals=0)
SMALL = pltpu.CompilerParams(vmem_limit_bytes=10 * MIB)


def factors(mesh):
    seq, mp = mesh.shape["seq"], mesh.shape["mp"]
    along_y = 1
    while 2 * along_y * along_y < seq:
        along_y *= 2
    return seq // along_y, along_y, mp // 2, 2


def rotate(value, axis, by):
    size = lax.axis_size(axis)
    return lax.ppermute(value, axis, [(i, (i + by) % size) for i in range(size)])


class Steps:
    def __init__(self):
        self.gate, self.open = (), []

    def __call__(self, send, value, *earlier, wait=True):
        found = send(after(value, *self.gate, *earlier))
        if wait:
            self.open.append(found)
        return found

    def then(self, *others):
        self.gate, self.open = tuple(self.open) + others, []


def after(value, *earlier):
    return lax.optimization_barrier((value, *earlier))[0]


def split_kernel(source, gain, target):
    target[0] = (source[0, 0].astype(jnp.float32) * gain[...]).astype(jnp.bfloat16)


def split_weights(in_weight, block, c, gain):
    parts = lax.axis_size("z")
    rows, columns = in_weight.shape[2], in_weight.shape[3] // parts
    if columns % 128:
        scaled = (in_weight[block, c].astype(jnp.float32) * gain).astype(jnp.bfloat16)
        return scaled.reshape(rows, parts, columns).transpose(1, 0, 2)
    return pl.pallas_call(
        split_kernel,
        grid=(parts,),
        in_specs=[
            pl.BlockSpec((1, 1, rows, columns), lambda k: (block, c, 0, k)),
            pl.BlockSpec((rows, 1), lambda k: (0, 0)),
        ],
        out_specs=pl.BlockSpec((1, rows, columns), lambda k: (k, 0, 0)),
        cost_estimate=SHORT_CALL,
        compiler_params=pltpu.CompilerParams(vmem_limit_bytes=10 * MIB),
        out_shape=jax.ShapeDtypeStruct((parts, rows, columns), jnp.bfloat16),
    )(in_weight, gain)


def exchange(pieces):
    return lax.all_to_all(pieces, "z", 0, 0, tiled=True)


def others(axis, value, send):
    moves = [functools.partial(rotate, axis=axis, by=j) for j in range(1, lax.axis_size(axis))]
    return [value] + [send(move, value) for move in moves]


def at_once(move, value):
    return move(value)


def slot_of(z_from, x_at, c_at):
    x_size, c_size = lax.axis_size("x"), lax.axis_size("c")
    x_from, c_from = z_from // c_size, z_from % c_size
    return ((x_at - x_from) % x_size) * c_size + (c_at - c_from) % c_size


def joined_kernel(blocks, cuts, place_ref, tokens_ref, *refs):
    firsts, rows = refs[:blocks], refs[blocks:-5]
    out_ref, first_held, rows_held, first_came, rows_came = refs[-5:]
    parts = place_ref.shape[0] // 2
    y_size = len(rows) // cuts // parts
    deep = rows[0].shape[0]

    def first_arrival(r):
        return pltpu.make_async_copy(firsts[r], first_held.at[r], first_came.at[r])

    def rows_arrival(n):
        return pltpu.make_async_copy(rows[n], rows_held.at[n], rows_came.at[n])

    for r in range(blocks):
        first_arrival(r).start()
    for n in range(len(rows)):
        rows_arrival(n).start()
    for r in range(blocks):
        first_arrival(r).wait()
    total = tokens_ref[...].astype(jnp.float32)
    for n in range(len(rows)):
        rows_arrival(n).wait()
        begin = pl.multiple_of((place_ref[parts + n // cuts % y_size] * cuts + n % cuts) * deep, deep)
        total = total + jnp.dot(
            first_held[place_ref[n // cuts // y_size], :, pl.ds(begin, deep)], rows_held[n], preferred_element_type=jnp.float32
        )
    out_ref[...] = total.astype(out_ref.dtype)


def joined(tokens, first, held, places, where):
    _, y_at, x_at, c_at = where
    parts, y_size = len(held), len(held[0][0])
    place = [slot_of(p, x_at, c_at) for p in places] + [(y_at - j) % y_size for j in range(y_size)]
    place += [y_at * 0] * (2 * parts - len(place))
    rows = [half[j] for group in held for j in range(y_size) for half in group]
    anywhere = pl.BlockSpec(memory_space=pl.ANY)
    return pl.pallas_call(
        functools.partial(joined_kernel, len(first), len(held[0])),
        grid_spec=pltpu.PrefetchScalarGridSpec(
            num_scalar_prefetch=1,
            grid=(1,),
            in_specs=[pl.BlockSpec(tokens.shape, lambda i, place: (0, 0))] + [anywhere] * (len(first) + len(rows)),
            out_specs=pl.BlockSpec(tokens.shape, lambda i, place: (0, 0)),
            scratch_shapes=[
                pltpu.VMEM((len(first),) + first[0].shape, jnp.bfloat16),
                pltpu.VMEM((len(rows),) + rows[0].shape, jnp.bfloat16),
                pltpu.SemaphoreType.DMA((len(first),)),
                pltpu.SemaphoreType.DMA((len(rows),)),
            ],
        ),
        out_shape=jax.ShapeDtypeStruct(tokens.shape, tokens.dtype),
        compiler_params=pltpu.CompilerParams(vmem_limit_bytes=60 * MIB),
    )(jnp.stack(place).astype(jnp.int32), tokens, *first, *rows)


def all_of_c(found):
    return [rotate(p, "c", d) if d else p for p in found for d in range(lax.axis_size("c"))]


def next_along_z(value):
    return rotate(value, "z", 1)


def project_kernel(groups, kept, order_ref, *refs):
    count = len(refs) - 5
    pieces = refs[: count - 3 * (order_ref.shape[0] - groups[1])]
    weights = refs[len(pieces) : count]
    out_ref, held, total, squares, arrived = refs[-5:]
    step = pl.program_id(0)
    y_size = len(weights) // 3
    deep, width = weights[0].shape[1], weights[0].shape[2]
    rows = pieces[0].shape[0]

    def arrival(g, r):
        return pltpu.make_async_copy(
            pieces[g * groups[1] + r], held.at[r, pl.ds(g * rows, rows)], arrived.at[r, g]
        )

    @pl.when(step == 0)
    def _():
        for r in range(groups[1]):
            for g in range(groups[0]):
                arrival(g, r).start()
        total[...] = jnp.zeros_like(total)
        squares[...] = jnp.zeros_like(squares)

    for r in range(groups[1]):

        @pl.when(step == r)
        def _(r=r):
            for g in range(groups[0]):
                arrival(g, r).wait()

    for g in range(groups[0]):
        these = slice(g * rows, (g + 1) * rows)
        values = held[step, these].astype(jnp.float32)
        squares[these] += jnp.sum(values * values, axis=1, keepdims=True)
    for c in range(3):
        some = 0.0
        for j in range(y_size):
            begin = pl.multiple_of(order_ref[groups[1] + j] * deep, deep)
            some = some + jnp.dot(
                held[step, :, pl.ds(begin, deep)], weights[c * y_size + j][order_ref[step] if kept else 0], preferred_element_type=jnp.float32
            )
        total[:, c * width : (c + 1) * width] += some

    @pl.when(step == groups[1] - 1)
    def _():
        scale = lax.rsqrt(squares[...] / (groups[1] * pieces[0].shape[1]) + 1e-06)
        out_ref[...] = (total[...] * scale).astype(out_ref.dtype)


def project(found, weights, order, kept=False):
    groups = (len(found), len(found[0]))
    flat = [w for group in weights for w in group]
    pieces = [p for group in found for p in group]
    rows, features_here = pieces[0].shape
    width = flat[0].shape[2]
    needed = groups[0] * rows * (groups[1] * features_here * 2 + 3 * width * 8 + 512) + 12 * flat[0][0].size * len(flat) // 3
    out = pl.pallas_call(
        functools.partial(project_kernel, groups, kept),
        grid_spec=pltpu.PrefetchScalarGridSpec(
            num_scalar_prefetch=1,
            grid=(groups[1],),
            in_specs=[pl.BlockSpec(memory_space=pl.ANY)] * len(pieces)
            + [
                pl.BlockSpec(memory_space=pltpu.VMEM)
                if kept
                else pl.BlockSpec((1,) + w.shape[1:], lambda r, order: (order[r], 0, 0))
                for w in flat
            ],
            out_specs=pl.BlockSpec((groups[0] * rows, 3 * width), lambda r, order: (0, 0)),
            scratch_shapes=[
                pltpu.VMEM((groups[1], groups[0] * rows, features_here), jnp.bfloat16),
                pltpu.VMEM((groups[0] * rows, 3 * width), jnp.float32),
                pltpu.VMEM((groups[0] * rows, 1), jnp.float32),
                pltpu.SemaphoreType.DMA((groups[1], groups[0])),
            ],
        ),
        out_shape=jax.ShapeDtypeStruct((groups[0] * rows, 3 * width), jnp.bfloat16),
        compiler_params=pltpu.CompilerParams(vmem_limit_bytes=(30 * MIB) if kept else 60 * MIB),
    )(order, *pieces, *flat)
    return out.reshape(groups[0], rows, 3 * width)


def mix_table(z_at, y_at, places):
    parts = len(places)
    stacked = jnp.stack(places)
    behind = jnp.where(y_at == 0, stacked[(stacked - 1) % parts], jnp.arange(parts))
    some = jnp.where((y_at == 0) & (stacked == 0), 0, 1)
    return jnp.stack([behind, some, stacked]).astype(jnp.int32)


def delayed(value, by):
    return pltpu.roll(value, by, 0) if by else value


def taps_sum(value, taps):
    total = taps[0] * value
    for s in range(1, len(taps)):
        total = total + taps[s] * delayed(value, s)
    return total


def features(lanes, width, start, table_ref, proj_ref, before_ref, feat_ref):
    some = table_ref[1, pl.program_id(0)].astype(jnp.float32)
    out = []
    for c in range(3):
        begin = c * width + start
        before = before_ref[0, :, begin : begin + lanes].astype(jnp.float32) * some
        value = jnp.concatenate([before, proj_ref[0, :, begin : begin + lanes].astype(jnp.float32)], axis=0)
        taps = [feat_ref[c, s : s + 1, start : start + lanes] for s in range(feat_ref.shape[1])]
        out.append(taps_sum(value, taps))
    return out


def short_kernel(table_ref, proj_ref, before_ref, feat_ref, taps_ref, out_ref):
    width = out_ref.shape[2]
    lanes = min(128, width)
    rim = before_ref.shape[1]
    for start in range(0, width, lanes):
        query, key, value = features(lanes, width, start, table_ref, proj_ref, before_ref, feat_ref)
        kv = (key * value).astype(jnp.bfloat16).astype(jnp.float32)
        taps = [taps_ref[s : s + 1, start : start + lanes] for s in range(taps_ref.shape[0])]
        inner = taps_sum(kv, taps)
        out_ref[0, :, start : start + lanes] = (query[rim:] * inner[rim:]).astype(out_ref.dtype)


def gate_kernel(table_ref, proj_ref, before_ref, feat_ref, query_ref, kv_ref):
    width = kv_ref.shape[2]
    lanes = min(128, width)
    rim = before_ref.shape[1]
    for start in range(0, width, lanes):
        query, key, value = features(lanes, width, start, table_ref, proj_ref, before_ref, feat_ref)
        query_ref[0, :, start : start + lanes] = query[rim:]
        kv_ref[0, :, start : start + lanes] = (key[rim:] * value[rim:]).astype(kv_ref.dtype)


def medium_kernel(table_ref, query_ref, kv_ref, before_ref, matrix_ref, out_ref):
    groups, span = matrix_ref.shape[0], matrix_ref.shape[1]
    count, width = out_ref.shape[1], out_ref.shape[2]
    lanes = min(128, width)
    per_group = width // groups
    some = table_ref[1, pl.program_id(0)]
    before = before_ref[0]
    before = jnp.where(some > 0, before, jnp.zeros_like(before))
    lane = lax.broadcasted_iota(jnp.int32, (span, lanes), 1) // per_group
    for block in range(count // span):
        own = kv_ref[0, block * span : (block + 1) * span]
        pair = jnp.concatenate([before, own], axis=0)
        before = own
        rows = slice(block * span, (block + 1) * span)
        for start in range(0, width, lanes):
            inner = jnp.zeros((span, lanes), jnp.float32)
            for g in range(lanes // per_group):
                taken = jnp.dot(
                    matrix_ref[start // per_group + g], pair[:, start : start + lanes], preferred_element_type=jnp.float32
                )
                inner = jnp.where(lane == g, taken, inner)
            query = query_ref[0, rows, start : start + lanes]
            out_ref[0, rows, start : start + lanes] = (query * inner).astype(out_ref.dtype)


def whole_spec(value):
    return pl.BlockSpec(value.shape, lambda i, table: (0,) * value.ndim)


def piece_spec(value, which=None):
    def index(i, table):
        return (i if which is None else table[which, i], 0, 0)

    return pl.BlockSpec((1,) + value.shape[1:], index)


def tails(pieces, count):
    return rotate(pieces[:, pieces.shape[1] - count :], "y", 1)


def short_mix(proj, before, feat, taps, table):
    out = jax.ShapeDtypeStruct(proj.shape[:2] + (proj.shape[2] // 3,), jnp.bfloat16)
    return pl.pallas_call(
        short_kernel,
        grid_spec=pltpu.PrefetchScalarGridSpec(
            num_scalar_prefetch=1,
            grid=(proj.shape[0],),
            in_specs=[piece_spec(proj), piece_spec(before, 0), whole_spec(feat), whole_spec(taps)],
            out_specs=piece_spec(out),
        ),
        cost_estimate=SHORT_CALL,
        compiler_params=SMALL,
        out_shape=out,
    )(table, proj, before, feat, taps)


def gate(proj, before, feat, table):
    shape = proj.shape[:2] + (proj.shape[2] // 3,)
    query = jax.ShapeDtypeStruct(shape, jnp.float32)
    kv = jax.ShapeDtypeStruct(shape, jnp.bfloat16)
    return pl.pallas_call(
        gate_kernel,
        grid_spec=pltpu.PrefetchScalarGridSpec(
            num_scalar_prefetch=1,
            grid=(proj.shape[0],),
            in_specs=[piece_spec(proj), piece_spec(before, 0), whole_spec(feat)],
            out_specs=[piece_spec(query), piece_spec(kv)],
        ),
        cost_estimate=SHORT_CALL,
        compiler_params=SMALL,
        out_shape=[query, kv],
    )(table, proj, before, feat)


def medium_early(early, feat, table, span):
    near = tails(early, 16)
    query, kv = gate(early, near, feat, jnp.minimum(table[:, :-1], table.shape[1] - 2))
    return near, query, kv, tails(kv, span)


def medium_mix(early, made_early, last, feat, matrix, table, z_at):
    parts, span = table.shape[1], matrix.shape[1]
    near_early, query, kv, far_early = made_early
    near = jnp.concatenate([near_early, tails(last, 16)])
    close = medium(after(query, last), kv, far_early, matrix, table[:, : parts - 2])
    both = after(jnp.concatenate([early[-1:], last]), close)
    query, kv = gate(both, near, feat, table[:, parts - 2 :])
    far = jnp.concatenate([far_early, tails(kv[1:], span)])
    distant = medium(query, kv, far, matrix, table[:, parts - 2 :])
    return home([close[k] for k in range(parts - 2)] + [distant[0], distant[1]], z_at)


def medium(query, kv, before, matrix, table):
    count = table.shape[1]
    shape = (count,) + kv.shape[1:]
    return pl.pallas_call(
        medium_kernel,
        grid_spec=pltpu.PrefetchScalarGridSpec(
            num_scalar_prefetch=1,
            grid=(count,),
            in_specs=[piece_spec(query), piece_spec(kv), piece_spec(before, 0), whole_spec(matrix)],
            out_specs=piece_spec(kv),
        ),
        cost_estimate=SHORT_CALL,
        compiler_params=SMALL,
        out_shape=jax.ShapeDtypeStruct(shape, jnp.bfloat16),
    )(table, query, kv, before, matrix)


def toeplitz_kernel(row_ref, out_ref):
    width = out_ref.shape[1]
    rows = jnp.broadcast_to(row_ref[0], (width, 3 * width))
    turned = pltpu.roll(rows, 0, 1, stride=1, stride_axis=0)
    out_ref[0] = turned[:, : 2 * width].astype(out_ref.dtype)


def toeplitz(filt):
    groups, width = filt.shape
    row = jnp.concatenate([jnp.zeros((groups, 1)), filt[:, ::-1], jnp.zeros((groups, 2 * width - 1))], axis=1)[:, None]
    return pl.pallas_call(
        toeplitz_kernel,
        grid=(groups,),
        in_specs=[pl.BlockSpec((1, 1, 3 * width), lambda g: (g, 0, 0))],
        out_specs=pl.BlockSpec((1, width, 2 * width), lambda g: (g, 0, 0)),
        cost_estimate=SHORT_CALL,
        compiler_params=SMALL,
        out_shape=jax.ShapeDtypeStruct((groups, width, 2 * width), jnp.bfloat16),
    )(row)


def channels_of(value, z_at, axis):
    size = value.shape[axis] // lax.axis_size("z")
    return lax.dynamic_slice_in_dim(value, z_at * size, size, axis)


def home(pieces, z_at):
    parts = len(pieces)
    stacked = jnp.stack([rotate(piece, "z", -k) if k else piece for k, piece in enumerate(pieces)])
    ordered = [lax.dynamic_index_in_dim(stacked, (k - z_at) % parts, 0, keepdims=False) for k in range(parts)]
    return jnp.concatenate(ordered, axis=1)


def local(tokens, norm_gain, in_weight, feat_filter, short_filter, medium_filter, out_weight):
    where = tuple(lax.axis_index(a) for a in AXES)
    z_at, y_at, x_at, c_at = where
    parts = lax.axis_size("z")
    rows = in_weight.shape[2]
    width = in_weight.shape[3] // parts
    begin = (z_at * lax.axis_size("y") + y_at) * rows
    gains = lax.dynamic_slice_in_dim(norm_gain, begin, rows, 1)[:, :, None]
    feat = channels_of(feat_filter, z_at, 3)
    short = channels_of(short_filter, z_at, 0)
    short_taps = jnp.repeat(short.T, width // short.shape[0], axis=1)
    matrix = toeplitz(channels_of(medium_filter, z_at, 0))
    places = [(z_at - k) % parts for k in range(parts)]
    table = mix_table(z_at, y_at, places)
    x_size, c_size, y_size = (lax.axis_size(a) for a in ("x", "c", "y"))
    order = [((x_at - d) % x_size) * c_size + (c_at - e) % c_size for d in range(x_size) for e in range(c_size)]
    order = jnp.stack(order + [(y_at - j) % y_size for j in range(y_size)]).astype(jnp.int32)

    def split(block, c):
        return split_weights(in_weight, block, c, gains[block])

    step = Steps()
    ring, found, came, weights = [tokens], [], [], []
    rows_ring, held = [jnp.split(out_weight, 1 if out_weight.shape[0] % 256 else 2)], []
    splits = [[split(block, c) for c in range(3)] for block in range(2)]
    for k in range(parts):
        if k < parts - 1:
            ring.append(next_along_z(ring[k]))
        found.append([others("c", ring[k], step)])
        fresh = others("x", ring[k], step)[1:]
        own = found[k][0][1:]
        if k < 3:
            came.append(exchange(after(splits[0][k], *own, *came[-1:])))
        if k:
            found[k - 1] += [others("c", piece, step) for piece in waiting]
        waiting = fresh
        if k == 0:
            held.append([others("y", half, step) for half in rows_ring[0]])
        elif k <= 3:
            weights.append(others("y", after(came[k - 1], *own), step))
        if k == parts - 1:
            rows_ring.append([step(next_along_z, after(half, came[2])) for half in rows_ring[0]])
        step.then(*([splits[0][1:], splits[1] + [matrix], []] + [[]] * parts)[k])
    found[-1] += [others("c", piece, at_once) for piece in waiting]
    proj = project([sum(group, []) for group in found], weights, order)
    near = tails(proj, 16)
    for k in range(1, parts - 1):
        rows_ring.append([next_along_z(half) for half in rows_ring[k]])
        held.append([])
        for half in rows_ring[k]:
            held[k].append(others("y", after(half, near) if k == parts - 2 else half, at_once))
        if k == 1:
            near = after(near, *rows_ring[-1], *sum(held[1], []))
    gated = short_mix(proj, near, feat[0], short_taps, table)
    gated = after(gated, *rows_ring[-1], *sum(held[-1], []))
    back = home([gated[k] for k in range(parts)], z_at)
    held.append([others("y", after(half, *sum(held[-1], [])), at_once) for half in rows_ring[-1]])
    first = all_of_c([after(piece, *sum(held[-1], [])) for piece in others("x", back, at_once)])
    step.then(gated)
    step.then(*step.gate, back)
    came, weights_next = [step(exchange, splits[1][0])], []
    came.append(exchange(after(splits[1][1], came[0], *first)))
    stream = joined(tokens, first, held, places, where)

    step.then(stream)
    ring, found, swapped = [stream], [], []

    def swap(k):
        found.append([others("c", ring[k], step)])
        swapped.append(others("x", ring[k], step)[1:])

    def spread(k):
        found[k] += [others("c", piece, step) for piece in swapped[k]]

    ring.append(step(next_along_z, ring[0]))
    weights_next.append(others("y", came[0], step))
    swap(0)
    step.then()
    came.append(step(exchange, splits[1][2]))
    weights_next.append(others("y", came[1], step))
    swap(1)
    spread(0)
    step.then()
    for k in range(2, parts):
        ring.append(step(next_along_z, ring[k - 1]))
        if k == 2:
            weights_next.append(others("y", came[2], functools.partial(step, wait=False)))
        else:
            swap(k - 1)
        spread(k - 1 if k == 2 else k - 2) if k != 3 else None
        step.then()
    early = project([sum(group, []) for group in found[:2]], weights_next, order)
    step.then(*step.gate, early)
    spread(parts - 2)
    count = stream.shape[0]
    half = count // 2
    near_half = others("x", ring[-1][:half], step)[1:]
    far_half = [step(next_along_z, piece[half:]) for piece in swapped[-1]]
    halves = [[others("c", ring[-1][:half], at_once)], [others("c", ring[-1][half:], at_once)]]
    early = [early] + [project([sum(group, [])], weights_next, order, True) for group in found[2:]]
    early = jnp.concatenate(early)
    for group, more in zip(halves, (near_half, far_half)):
        group += [others("c", after(piece, early), at_once) for piece in more]
    made_early = medium_early(early, feat[1], table, matrix.shape[1])
    halves[0][0][0] = after(halves[0][0][0], made_early[2])
    last = project([sum(group, []) for group in halves], weights_next, order, True).reshape(1, count, -1)
    return stream, medium_mix(early, made_early, last, feat[1], matrix, table, z_at)


def solution(mesh):
    wide = Mesh(mesh.devices.reshape(factors(mesh)), AXES)
    seq, mp = ("z", "y"), ("x", "c")
    placed = (
        P(seq, mp),
        P(),
        P(None, None, seq, mp),
        P(None, None, None, mp),
        P(mp, None),
        P(mp, None),
        P(seq, mp),
    )
    return jax.shard_map(
        local,
        mesh=wide,
        in_specs=placed,
        out_specs=(P(seq, mp), P(seq, mp)),
        check_vma=False,
    )
```
